32 devices in a mesh: shift: 4 (over z), leaf: 8 (over y, x, core).
Axes of the slice: x: 2, y: 2, z: 4, core: 2. Of those that a mesh axis runs over, the one named last changes fastest.
Arguments:
- leaf_rhs: bfloat16 [8, 1024, 1024], P('leaf'), may hold values from -6 to 6
- leaf_inverse: bfloat16 [4, 8, 1024, 1024], P('shift', 'leaf')
- leaf_coupling: bfloat16 [4, 8, 1024, 384], P('shift', 'leaf'), may hold values from -0.1875 to 0.1875
- leaf_rows: int32 [8, 384], P('leaf'), may hold values from 0 to 767, as said below
- front_sizes: int32 [3], replicated, may hold values from 384 to 768, as said below
- front_inverse: bfloat16 [4, 3, 8, 768, 768], P('shift', None, 'leaf'), as said below
- front_coupling: bfloat16 [4, 2, 8, 768, 768], P('shift', None, 'leaf'), as said below
- shift_weight: float32 [4], P('shift'), may hold values from -1 to 1
Outputs:
- filtered: float32 [8, 1024, 1024], P('leaf', 'shift')
The draws below stay inside these ranges and needn't reach their ends.
Inputs may be any that keep to these rules, and one draw needn't show every extreme that they name: `leaf_rows`: the 384 entries of one leaf are distinct. `front_sizes`: the front of at least one level is full. `front_inverse`: all leaves below one separator hold the same front inverse for it. `front_coupling`: all leaves below one separator hold the same coupling for it.
All inputs are finite; a program needn't handle non-finite values.
Results may differ from the reference program's by a relative error of at most 0.01.
Values may be sent and summed in bfloat16 or wider, within the bound.
No kernel may reach another device: no remote copies, remote signals or barrier semaphores. Data moves between devices by JAX's collectives and lax.ppermute only.
A program may use at most 128 MiB of HBM per device.

```python
import math
import jax
import jax.numpy as jnp
from jax import lax

L = 1024
FRONT = 768
COLS = 1024
BND = 384
LEAVES = 8
SHIFTS = 4
LEVELS = 3


def rough_noise(key, array_shape):
    return jax.random.normal(key, array_shape, jnp.float32)


def draw_leaf_inverse(key, part):
    diagonal = jax.random.uniform(jax.random.fold_in(key, 11), (SHIFTS, LEAVES, L), jnp.float32, 0.5, 1.5)
    noise = rough_noise(jax.random.fold_in(key, 12), (SHIFTS, LEAVES, L, L)) * (0.5 / math.sqrt(L))
    return (noise + diagonal[..., None] * jnp.eye(L, dtype=jnp.float32)).astype(jnp.bfloat16)


def draw_front_inverse(key, part):
    stacked = []
    for level_index in range(LEVELS):
        stride = 2 ** (level_index + 1)
        node_count = LEAVES // stride
        level_key = jax.random.fold_in(key, 100 + level_index)
        diagonal = jax.random.uniform(jax.random.fold_in(level_key, 1), (SHIFTS, node_count, FRONT), jnp.float32, 0.4, 1.0)
        noise = rough_noise(jax.random.fold_in(level_key, 2), (SHIFTS, node_count, FRONT, FRONT)) * (0.3 / math.sqrt(FRONT))
        block = (noise + diagonal[..., None] * jnp.eye(FRONT, dtype=jnp.float32)).astype(jnp.bfloat16)
        stacked.append(jnp.repeat(block, stride, axis=1))
    return jnp.stack(stacked, axis=1)


def draw_front_coupling(key, part):
    stacked = []
    for level_index in range(LEVELS - 1):
        stride = 2 ** (level_index + 1)
        node_count = LEAVES // stride
        level_key = jax.random.fold_in(key, 200 + level_index)
        block = (rough_noise(level_key, (SHIFTS, node_count, FRONT, FRONT)) / math.sqrt(FRONT)).astype(jnp.bfloat16)
        stacked.append(jnp.repeat(block, stride, axis=1))
    return jnp.stack(stacked, axis=1)


def draw_leaf_rows(key, part):
    scores = jax.random.randint(jax.random.fold_in(key, 31), (LEAVES, FRONT), 0, 2 ** 20) * FRONT
    scores = scores + jnp.arange(FRONT, dtype=jnp.int32)[None, :]
    scores = scores.at[0, 0].set(-2).at[0, FRONT - 1].set(-1)
    ordering = jnp.argsort(scores, axis=1, stable=True)
    return ordering[:, :BND].astype(jnp.int32)


def draw_front_sizes(key, part):
    sizes = jax.random.randint(jax.random.fold_in(key, 41), (LEVELS,), FRONT // 2, FRONT + 1)
    chosen = jax.random.randint(jax.random.fold_in(key, 42), (), 0, LEVELS)
    return jnp.where(jnp.arange(LEVELS) == chosen, FRONT, sizes).astype(jnp.int32)


def shard_levels(own_key, shape, cuts, smallest, largest):
    level, own = 1.0, jax.random.fold_in(own_key, 6)
    for axis_at, blocks in cuts:
        steps = jnp.exp(jax.random.uniform(jax.random.fold_in(own, axis_at), (blocks,), jnp.float32, smallest / len(cuts), largest / len(cuts)))
        level = level * jnp.repeat(steps, shape[axis_at] // blocks).reshape([-1 if axis == axis_at else 1 for axis in range(len(shape))])
    return level


def bell_draw(key, shape, scale, reach, cuts=(), kind=jnp.bfloat16):
    drawn = scale * jax.random.normal(key, shape, jnp.float32)
    if cuts:
        drawn = drawn * shard_levels(key, shape, cuts, -0.22, 0.18)
    return jnp.clip(drawn, -reach, reach).astype(kind)


def setup_inputs(seed: int = 0) -> dict:
    streams_of = jax.random.split(jax.random.key(seed), 9)
    return {
        "leaf_rhs": bell_draw(streams_of[0], (LEAVES, L, COLS), 1.0, 6.0, ((0, 8),)),
        "leaf_inverse": draw_leaf_inverse(jax.random.fold_in(streams_of[8], 71), 0),
        "leaf_coupling": bell_draw(streams_of[2], (SHIFTS, LEAVES, L, BND), L ** -0.5, 0.1875, ((0, 4), (1, 8))),
        "leaf_rows": draw_leaf_rows(jax.random.fold_in(streams_of[8], 71), 0),
        "front_sizes": draw_front_sizes(jax.random.fold_in(streams_of[8], 71), 0),
        "front_inverse": draw_front_inverse(jax.random.fold_in(streams_of[8], 71), 0),
        "front_coupling": draw_front_coupling(jax.random.fold_in(streams_of[8], 71), 0),
        "shift_weight": jnp.clip(jax.random.uniform(streams_of[7], (SHIFTS,), jnp.float32, -1.0, 1.0) * shard_levels(streams_of[7], (SHIFTS,), ((0, 4),), -0.4, 0.0), -1.0, 1.0),
    }


def reference(leaf_rhs, leaf_inverse, leaf_coupling, leaf_rows, front_sizes, front_inverse, front_coupling, shift_weight):
    front_index = jnp.arange(FRONT, dtype=jnp.int32)[:, None]
    accumulated = jnp.zeros((LEAVES, L, COLS), jnp.float32)
    for shift_index in range(SHIFTS):
        def leaf_up(leaf_index):
            leaf_half = jnp.dot(leaf_inverse[shift_index, leaf_index], leaf_rhs[leaf_index], preferred_element_type=jnp.float32).astype(jnp.bfloat16)
            boundary = jnp.dot(leaf_coupling[shift_index, leaf_index].T, leaf_half, preferred_element_type=jnp.float32)
            placed = jnp.zeros((FRONT, COLS), jnp.float32).at[leaf_rows[leaf_index]].add(boundary)
            return leaf_half, placed

        leaf_halves, placed_all = lax.map(leaf_up, jnp.arange(LEAVES, dtype=jnp.int32))
        gathered = placed_all.reshape(LEAVES // 2, 2, FRONT, COLS).sum(axis=1)
        solved_list = []
        mask_list = []
        for level_index in range(LEVELS):
            stride = 2 ** (level_index + 1)
            live_rows = front_index < front_sizes[level_index]
            inverse = front_inverse[shift_index, level_index, ::stride].astype(jnp.float32)
            operand = jnp.where(live_rows, gathered, 0.0).astype(jnp.bfloat16)
            operand = lax.optimization_barrier(operand).astype(jnp.float32)
            solved = jnp.where(live_rows, jnp.einsum('nij,njc->nic', inverse, operand), 0.0).astype(jnp.bfloat16)
            solved_list.append(solved)
            mask_list.append(live_rows)
            if level_index < LEVELS - 1:
                coupling = front_coupling[shift_index, level_index, ::stride].astype(jnp.float32)
                raised = jnp.einsum('nij,nic->njc', coupling, solved.astype(jnp.float32))
                gathered = raised.reshape(raised.shape[0] // 2, 2, FRONT, COLS).sum(axis=1)
        current = solved_list[-1]
        for level_index in range(LEVELS - 2, -1, -1):
            stride = 2 ** (level_index + 1)
            inverse = front_inverse[shift_index, level_index, ::stride].astype(jnp.float32)
            coupling = front_coupling[shift_index, level_index, ::stride].astype(jnp.float32)
            parent = jnp.repeat(current, 2, axis=0).astype(jnp.float32)
            lifted = jnp.einsum('nij,njc->nic', coupling, parent).astype(jnp.bfloat16)
            lifted = lax.optimization_barrier(lifted).astype(jnp.float32)
            correction = jnp.einsum('nij,njc->nic', inverse, lifted)
            current = jnp.where(mask_list[level_index], solved_list[level_index].astype(jnp.float32) - correction, 0.0).astype(jnp.bfloat16)
        parents = jnp.repeat(current, 2, axis=0)

        def leaf_down(leaf_index):
            picked = parents[leaf_index][leaf_rows[leaf_index]]
            lifted = jnp.dot(leaf_coupling[shift_index, leaf_index], picked, preferred_element_type=jnp.float32).astype(jnp.bfloat16)
            solution = leaf_halves[leaf_index].astype(jnp.float32) - jnp.dot(leaf_inverse[shift_index, leaf_index], lifted, preferred_element_type=jnp.float32)
            return shift_weight[shift_index] * solution

        accumulated = accumulated + lax.map(leaf_down, jnp.arange(LEAVES, dtype=jnp.int32))
    return accumulated
```

```python
import functools

import jax
import jax.numpy as jnp
from jax import lax
from jax.experimental import pallas as pl
from jax.experimental.pallas import tpu as pltpu
from jax.sharding import PartitionSpec as P

WIDE = jnp.float32
NARROW = jnp.bfloat16
VMEM_LIMIT = 24 * 1024 * 1024
SHARES = (4, 4)
PARTS = ((4, 4), (4, 4))


COST = 0.01
TILES = 2


def exchange(value, axis, bit):
    mask = 2**bit
    pairs = [(source, source ^ mask) for source in range(lax.axis_size(axis))]
    return lax.ppermute(value, axis, pairs)


def dot(left, right, left_dim=1, right_dim=0):
    return lax.dot_general(
        left, right, (((left_dim,), (right_dim,)), ((), ())), preferred_element_type=WIDE
    )


class Chain:
    def __init__(self):
        self.last = None
        self.tag = None
        self.cost = COST

    def __call__(self, kernel, outs, scalars, arrays, name, far=(), out_space=pltpu.VMEM, scratch=()):
        after = [] if self.last is None else [self.last]

        def run(*refs):
            kernel(*refs[len(after) :])

        results = pl.pallas_call(
            run,
            out_shape=[jax.ShapeDtypeStruct(shape, kind) for shape, kind in outs],
            in_specs=[pl.BlockSpec(memory_space=pl.ANY)] * len(after)
            + [pl.BlockSpec(memory_space=pltpu.SMEM)] * len(scalars)
            + [pl.BlockSpec(memory_space=pltpu.VMEM)] * len(arrays)
            + [pl.BlockSpec(memory_space=pl.ANY)] * len(far),
            out_specs=[pl.BlockSpec(memory_space=out_space)] * len(outs),
            scratch_shapes=scratch,
            cost_estimate=pl.CostEstimate(
                flops=int(self.cost * 1.15e9), bytes_accessed=1, transcendentals=0
            ),
            compiler_params=pltpu.CompilerParams(vmem_limit_bytes=VMEM_LIMIT),
            name=self.tag + "_" + name,
        )(*after, *scalars, *arrays, *[pltpu.with_memory_space_constraint(a, pltpu.HBM) for a in far])
        self.last = results[0]
        return results


def live(value, size):
    unknowns = lax.broadcasted_iota(jnp.int32, value.shape, 1)
    return jnp.where(unknowns < size, value, 0.0)


def selector(rows, front):
    at = lax.broadcasted_iota(jnp.int32, (front, rows.shape[1]), 0)
    return (at == rows[...]).astype(WIDE).astype(NARROW)


def load_kernel(width, place, rhs_in, inverse_in, coupling_in, rows_in, fronts_in, links_in, *refs):
    front_in, link_in = fronts_in.at[0], links_in.at[0]
    own, other, half, chosen, inverse, coupling, rhs, front, link, rows, sems = refs
    count = rhs.shape[1] // 2
    tile = inverse.shape[0] // TILES
    mine = place[0]
    copies = []

    def columns(side, start, size):
        return pl.ds(pl.multiple_of(side * count + start, 128), size)

    def load(source, target):
        copies.append(pltpu.make_async_copy(source, target, sems.at[len(copies)]))
        copies[-1].start()

    for side in (mine, 1 - mine):
        load(rhs_in.at[:, columns(side, 0, width)], rhs.at[:, columns(side, 0, width)])
    for number in range(TILES):
        block = pl.ds(number * tile, tile)
        load(inverse_in.at[block], inverse.at[block])
    load(rows_in, rows)
    load(coupling_in, coupling)
    load(front_in, front)
    load(link_in, link)
    if width < count:
        for side in (mine, 1 - mine):
            load(rhs_in.at[:, columns(side, width, count - width)], rhs.at[:, columns(side, width, count - width)])

    copies[0].wait()
    copies[1].wait()
    both = jnp.concatenate([rhs[:, columns(mine, 0, width)], rhs[:, columns(1 - mine, 0, width)]], axis=1)
    for number in range(TILES):
        copies[2 + number].wait()
        block = pl.ds(number * tile, tile)
        half[block, :] = dot(inverse[block, :], both).astype(NARROW)
    copies[2 + TILES].wait()
    selected = selector(rows, own.shape[1])
    chosen[...] = selected
    copies[3 + TILES].wait()
    boundary = dot(half[...], coupling[...], 0, 0).astype(NARROW)
    placed = dot(boundary, selected, 1, 1).astype(NARROW)
    own[...] = placed[:width]
    other[...] = placed[width:]
    for copy in copies[4 + TILES :]:
        copy.wait()


def leaf_up_kernel(offset, width, place, inverse, rhs, coupling, chosen, *refs):
    if len(refs) > 3:
        fronts_in, links_in, own, other, half, fronts, links, sems = refs
        copies = [
            pltpu.make_async_copy(source.at[pl.ds(1, target.shape[0])], target, sems.at[number])
            for number, (source, target) in enumerate(((fronts_in, fronts), (links_in, links)))
        ]
    else:
        own, other, half = refs
        copies = []
    for copy in copies:
        copy.start()
    count = rhs.shape[1] // 2
    mine = place[0]

    def columns(side):
        return rhs[:, pl.ds(pl.multiple_of(side * count + offset, 128), width)]

    both = jnp.concatenate([columns(mine), columns(1 - mine)], axis=1)
    product = dot(inverse[...], both).astype(NARROW)
    half[...] = product
    boundary = dot(product, coupling[...], 0, 0).astype(NARROW)
    placed = dot(boundary, chosen[...], 1, 1).astype(NARROW)
    own[...] = placed[:width]
    other[...] = placed[width:]
    for copy in copies:
        copy.wait()


def front_up_kernel(sizes, mine, received, front, link, carried, solved):
    gathered = mine[...].astype(WIDE) + received[...].astype(WIDE)
    operand = live(gathered, sizes[0]).astype(NARROW)
    result = live(dot(operand, front[...], 1, 1), sizes[0]).astype(NARROW)
    solved[...] = result
    carried[...] = dot(result, link[...]).astype(NARROW)


def product_kernel(sizes, front, link, fronts, links, downs, ups):
    downs[0] = dot(front[...], link[...]).astype(NARROW)
    for level in range(links.shape[0]):
        coupling = links[level]
        downs[level + 1] = dot(fronts[level], coupling).astype(NARROW)
        alive = lax.broadcasted_iota(jnp.int32, coupling.shape, 0) < sizes[level + 1]
        masked = jnp.where(alive, coupling, jnp.zeros_like(coupling))
        ups[level] = dot(fronts[level], masked, 0, 0).astype(NARROW)


def front_pass_kernel(level, sizes, mine, received, ups, carried, operand):
    gathered = mine[...].astype(WIDE) + received[...].astype(WIDE)
    value = live(gathered, sizes[level]).astype(NARROW)
    operand[...] = value
    carried[...] = dot(value, ups[level - 1]).astype(NARROW)


def front_solve_kernel(level, sizes, operand, fronts, solved):
    solved[...] = live(dot(operand[...], fronts[level - 1], 1, 1), sizes[level]).astype(NARROW)


def top_kernel(levels, sizes, mine, received, fronts, downs, *refs):
    *solved, back = refs
    gathered = mine[...].astype(WIDE) + received[...].astype(WIDE)
    operand = live(gathered, sizes[levels - 1]).astype(NARROW)
    current = live(dot(operand, fronts[levels - 2], 1, 1), sizes[levels - 1]).astype(NARROW)
    for level in range(levels - 2, -1, -1):
        correction = dot(current, downs[level], 1, 1)
        current = live(solved[level][...].astype(WIDE) - correction, sizes[level]).astype(NARROW)
    back[...] = current


def lift_kernel(inverse, coupling, lift):
    lift[...] = dot(inverse[...], coupling[...]).astype(NARROW)


def down(masks, place, weight, lift, picked, half, columns, out):
    block = out.shape[0] // len(masks)
    for number, mask in enumerate(masks):
        source = pl.ds(pl.multiple_of((place[1] ^ mask) * block, block), block)
        correction = dot(lift[source, :], picked, 1, 1)
        result = weight[0] * (half[source, columns].astype(WIDE) - correction)
        out[number * block : (number + 1) * block, :] = result.astype(out.dtype)


def down_first_kernel(masks, start, at, place, weight, lift, chosen, half, *refs):
    *backs, out, picked = refs
    width = out.shape[1]
    back = jnp.concatenate([ref[...] for ref in backs], axis=0)[at : at + width]
    values = dot(back, chosen[...]).astype(NARROW)
    picked[...] = values
    down(masks, place, weight, lift, values, half, pl.ds(start, width), out)


def down_second_kernel(masks, start, place, weight, lift, half, picked, out):
    down(masks, place, weight, lift, picked[...], half, pl.ds(start, out.shape[1]), out)


def add_kernel(kept, came, sent, rest):
    total = kept[...] + came[...].astype(WIDE)
    rows = sent.shape[0]
    sent[...] = total[:rows].astype(NARROW)
    rest[...] = total[rows:]


def last_add_kernel(kept, came, total):
    total[...] = kept[...] + came[...].astype(WIDE)


def body(
    leaf_rhs,
    leaf_inverse,
    leaf_coupling,
    leaf_rows,
    front_sizes,
    front_inverse,
    front_coupling,
    shift_weight,
):
    levels = lax.axis_size("leaf").bit_length() - 1
    shifts = lax.axis_size("shift")
    steps = shifts.bit_length() - 1
    core = lax.axis_index("leaf") & 1
    place = jnp.stack([core, lax.axis_index("shift")]).astype(jnp.int32)
    inverse_in, coupling_in, rhs_in = leaf_inverse[0, 0], leaf_coupling[0, 0], leaf_rhs[0]
    fronts_in, links_in = front_inverse[0, :, 0], front_coupling[0, :, 0]
    order, columns = rhs_in.shape
    front, boundary = fronts_in.shape[-1], coupling_in.shape[1]
    block = order // shifts
    unit = columns // (2 * sum(SHARES))
    widths = [share * unit for share in SHARES]
    offsets = [sum(widths[:n]) for n in range(len(widths))]
    def masks_of(step):
        if step == steps:
            return [0]
        stay = masks_of(step + 1)
        return [m | 1 << step for m in stay] + stay
    stay = masks_of(1)
    leave = [m | 1 for m in stay]

    chain = Chain()
    state = [dict() for _ in widths]
    final = [None for _ in widths]

    held = {}

    held = {}

    held = {}

    def leaf(n):
        width = widths[n]
        s = state[n]
        outs = [((width, front), NARROW)] * 2 + [((order, 2 * width), NARROW)]
        if n == 0:
            kept = {"inverse": inverse_in, "coupling": coupling_in, "rhs": rhs_in}
            shapes = [a.shape for a in kept.values()] + [(front, front)] * 2
            s["mine"], other, s["half"], held["chosen"], *loaded = chain(
                functools.partial(load_kernel, width),
                [*outs, ((front, boundary), NARROW), *[(shape, NARROW) for shape in shapes]],
                [place], [], "leaf_up", far=[rhs_in, inverse_in, coupling_in, leaf_rows, fronts_in, links_in],
                scratch=[pltpu.VMEM(leaf_rows.shape, jnp.int32), pltpu.SemaphoreType.DMA((8 + TILES,))],
            )
            held.update(zip([*kept, "front", "link"], loaded))
        else:
            far = [fronts_in, links_in] if n == 1 else []
            outs += [((a.shape[0] - 1, front, front), NARROW) for a in far]
            s["mine"], other, s["half"], *loaded = chain(
                functools.partial(leaf_up_kernel, offsets[n], width), outs, [place],
                [held[k] for k in ("inverse", "rhs", "coupling", "chosen")], "leaf_up",
                far=far, scratch=[pltpu.SemaphoreType.DMA((2,))] if far else [],
            )
            held.update(zip(("fronts", "links"), loaded))
        s["came"] = exchange(other, "leaf", 0)
        s["solved"] = []

    def up(n):
        width = widths[n]
        s = state[n]
        s["mine"], solved = chain(
            front_up_kernel, [((width, front), NARROW)] * 2, [front_sizes],
            [s["mine"], s["came"], held["front"], held["link"]], "front_up",
        )
        s["solved"].append(solved)
        s["came"] = exchange(s["mine"], "leaf", 1)

    def products():
        held["downs"], held["ups"] = chain(
            product_kernel,
            [((levels - 1, front, front), NARROW), ((levels - 2, front, front), NARROW)],
            [front_sizes], [held[k] for k in ("front", "link", "fronts", "links")], "products",
        )

    def middle(n):
        s = state[n]
        s["operands"] = []
        for level in range(1, levels - 1):
            s["mine"], operand = chain(
                functools.partial(front_pass_kernel, level), [((widths[n], front), NARROW)] * 2, [front_sizes],
                [s["mine"], s["came"], held["ups"]], "front_pass",
            )
            s["operands"].append(operand)
            s["came"] = exchange(s["mine"], "leaf", level + 1)

    def solve(n):
        s = state[n]
        for level in range(1, levels - 1):
            s["solved"] += chain(
                functools.partial(front_solve_kernel, level), [((widths[n], front), NARROW)], [front_sizes],
                [s["operands"][level - 1], held["fronts"]], "front_solve",
            )

    def top(n):
        s = state[n]
        (s["back"],) = chain(
            functools.partial(top_kernel, levels), [((widths[n], front), NARROW)], [front_sizes],
            [s["mine"], s["came"], held["fronts"], held["downs"], *s["solved"]], "top",
        )
        s["back_came"] = exchange(s["back"], "leaf", 0)

    def lift():
        (held["lift"],) = chain(
            lift_kernel, [((order, boundary), NARROW)], [], [held["inverse"], held["coupling"]], "lift"
        )

    def parts(n):
        sizes = [share * unit for share in PARTS[n]]
        return [(sum(sizes[:p]), size) for p, size in enumerate(sizes)]

    def first(n, part):
        s = state[n]
        start, width = parts(n)[part]
        backs, at = [s["back"], s["back_came"]], start
        if start + width <= widths[n]:
            backs = backs[:1]
        elif start >= widths[n]:
            backs, at = backs[1:], start - widths[n]
        sent, s["picked", part] = chain(
            functools.partial(down_first_kernel, leave, start, at),
            [((len(leave) * block, width), NARROW), ((width, boundary), NARROW)],
            [place, shift_weight],
            [held["lift"], held["chosen"], s["half"], *backs],
            "down_first",
        )
        s["sum_came", part] = exchange(sent, "shift", 0)

    def second(n, part):
        s = state[n]
        start, width = parts(n)[part]
        (s["kept", part],) = chain(
            functools.partial(down_second_kernel, stay, start),
            [((len(stay) * block, width), WIDE)],
            [place, shift_weight],
            [held["lift"], s["half"], s["picked", part]],
            "down_second",
        )

    def add(n, part):
        s = state[n]
        width = parts(n)[part][1]
        for step in range(1, steps):
            rows = block * (shifts >> step + 1)
            sent, s["kept", part] = chain(
                add_kernel, [((rows, width), NARROW), ((rows, width), WIDE)], [],
                [s["kept", part], s["sum_came", part]], "add",
            )
            s["sum_came", part] = exchange(sent, "shift", step)

    def last(n, part):
        s = state[n]
        (s["total", part],) = chain(
            last_add_kernel, [((block, parts(n)[part][1]), WIDE)], [],
            [s["kept", part], s["sum_came", part]], "last_add",
        )

    run = {
        "A": leaf,
        "B": up,
        "C": middle,
        "T": solve,
        "Q": lambda n: products(),
        "D": top,
        "G": lambda n: lift(),
        "E": first,
        "S": second,
        "F": add,
        "Z": last,
    }
    for step in ORDER:
        chain.tag, _, cost = step.partition(":")
        chain.cost = float(cost or COST)
        run[step[0]](*[int(digit) for digit in chain.tag[1:] or "0"])

    owned, others = [], []
    for n, width in enumerate(widths):
        whole = jnp.concatenate([state[n]["total", part] for part in range(len(PARTS[n]))], axis=1)
        owned.append(whole[:, :width])
        others.append(whole[:, width:])
    low = jnp.concatenate(owned + others, axis=1)
    high = jnp.concatenate(others + owned, axis=1)
    return jnp.where(core == 0, low, high)[None]


ORDER = ("A0", "A1", "B0", "G", "Q", "B1", "C0", "T0", "D0", "E00", "C1", "E01", "S00", "F00", "T1", "S01:2", "D1", "E10", "F01", "Z00", "S10:3", "E11", "F10", "S11", "Z01:2", "F11", "Z10", "Z11")


def solution(mesh):
    in_specs = (
        P("leaf", None, None),
        P("shift", "leaf", None, None),
        P("shift", "leaf", None, None),
        P("leaf", None),
        P(),
        P("shift", None, "leaf", None, None),
        P("shift", None, "leaf", None, None),
        P("shift"),
    )
    out_specs = P("leaf", "shift", None)
    return jax.shard_map(body, mesh=mesh, in_specs=in_specs, out_specs=out_specs, check_vma=False)
```

```python
import functools

import jax
import jax.numpy as jnp
from jax import lax
from jax.experimental import pallas as pl
from jax.experimental.pallas import tpu as pltpu
from jax.sharding import PartitionSpec as P

WIDE = jnp.float32
NARROW = jnp.bfloat16
VMEM_LIMIT = 24 * 1024 * 1024
SHARES = (1, 1, 2)
GROUPS = ((0, 1), (2,))
PARTS = ((((0, 0, 1), (1, 0, 1)),), (((0, 0, 1), (1, 0, 1)),), (((0, 0, 2),), ((1, 0, 2),)))
COST = 0.01
TILES = 2


def exchange(value, axis, bit):
    mask = 2**bit
    pairs = [(source, source ^ mask) for source in range(lax.axis_size(axis))]
    return lax.ppermute(value, axis, pairs)


def dot(left, right, left_dim=1, right_dim=0):
    return lax.dot_general(
        left, right, (((left_dim,), (right_dim,)), ((), ())), preferred_element_type=WIDE
    )


class Chain:
    def __init__(self):
        self.last = None
        self.tag = None
        self.cost = COST

    def __call__(self, kernel, outs, scalars, arrays, name, far=(), out_space=pltpu.VMEM, scratch=()):
        after = [] if self.last is None else [self.last]

        def run(*refs):
            kernel(*refs[len(after) :])

        results = pl.pallas_call(
            run,
            out_shape=[jax.ShapeDtypeStruct(shape, kind) for shape, kind in outs],
            in_specs=[pl.BlockSpec(memory_space=pl.ANY)] * len(after)
            + [pl.BlockSpec(memory_space=pltpu.SMEM)] * len(scalars)
            + [pl.BlockSpec(memory_space=pltpu.VMEM)] * len(arrays)
            + [pl.BlockSpec(memory_space=pl.ANY)] * len(far),
            out_specs=[pl.BlockSpec(memory_space=out_space)] * len(outs),
            scratch_shapes=scratch,
            cost_estimate=pl.CostEstimate(
                flops=int(self.cost * 1.15e9), bytes_accessed=1, transcendentals=0
            ),
            compiler_params=pltpu.CompilerParams(vmem_limit_bytes=VMEM_LIMIT),
            name=self.tag + "_" + name,
        )(*after, *scalars, *arrays, *[pltpu.with_memory_space_constraint(a, pltpu.HBM) for a in far])
        self.last = results[0]
        return results


def selector(rows, front):
    at = lax.broadcasted_iota(jnp.int32, (front, rows.shape[1]), 0)
    return (at == rows[...]).astype(WIDE).astype(NARROW)


def load_kernel(masks, width, rhs_in, inverse_in, coupling_in, rows_in, fronts_in, links_in, *refs):
    own, other, half, chosen, inverse, mixed, coupling, rhs, front, link, rows, sems = refs
    count = rhs.shape[1] // 2
    block = inverse.shape[0] // len(masks)
    core = lax.axis_index("leaf") & 1
    shift = lax.axis_index("shift")
    copies = []

    def load(source, target):
        copies.append(pltpu.make_async_copy(source, target, sems.at[len(copies)]))
        copies[-1].start()
        return copies[-1]

    def load_columns(start, size):
        return [
            load(
                rhs_in.at[:, pl.ds(pl.multiple_of(side * count + start, 128), size)],
                rhs.at[:, pl.ds(number * count + start, size)],
            )
            for number, side in enumerate((core, 1 - core))
        ]

    def load_blocks(source, target):
        return [
            load(
                source.at[pl.ds(pl.multiple_of((shift ^ mask) * block, block), block)],
                target.at[pl.ds(number * block, block)],
            )
            for number, mask in enumerate(masks)
        ]

    first = load_columns(0, width)
    blocks = load_blocks(inverse_in, inverse)
    small = [load(rows_in, rows)]
    small += load_blocks(coupling_in, mixed)

    for copy in first:
        copy.wait()
    both = jnp.concatenate([rhs[:, :width], rhs[:, count : count + width]], axis=1)
    parts = TILES
    for part in range(parts):
        for copy in blocks[part * len(blocks) // parts : (part + 1) * len(blocks) // parts]:
            copy.wait()
        if part == parts - 1:
            later = [load(fronts_in.at[0], front), load(links_in.at[0], link), load(coupling_in, coupling)]
            if width < count:
                later += load_columns(width, count - width)
        tile = pl.ds(part * (inverse.shape[0] // parts), inverse.shape[0] // parts)
        half[tile, :] = dot(inverse[tile, :], both).astype(NARROW)
    for copy in small:
        copy.wait()
    selected = selector(rows, own.shape[1])
    chosen[...] = selected
    boundary = dot(half[...], mixed[...], 0, 0).astype(NARROW)
    placed = dot(boundary, selected, 1, 1).astype(NARROW)
    own[...] = placed[:width]
    other[...] = placed[width:]
    for copy in later:
        copy.wait()


def leaf_up_kernel(offset, width, inverse, rhs, mixed, chosen, *refs):
    if len(refs) > 3:
        fronts_in, links_in, own, other, half, fronts, links, sems = refs
        copies = [
            pltpu.make_async_copy(source.at[pl.ds(1, target.shape[0])], target, sems.at[number])
            for number, (source, target) in enumerate(((fronts_in, fronts), (links_in, links)))
        ]
    else:
        own, other, half = refs
        copies = []
    for copy in copies:
        copy.start()
    count = rhs.shape[1] // 2
    both = jnp.concatenate(
        [rhs[:, offset : offset + width], rhs[:, count + offset : count + offset + width]], axis=1
    )
    product = dot(inverse[...], both).astype(NARROW)
    half[...] = product
    boundary = dot(product, mixed[...], 0, 0).astype(NARROW)
    placed = dot(boundary, chosen[...], 1, 1).astype(NARROW)
    own[...] = placed[:width]
    other[...] = placed[width:]
    for copy in copies:
        copy.wait()


def gather(level, mine, received, alive):
    total = mine.astype(WIDE) + received.astype(WIDE)
    return (total * alive[level : level + 1, :]).astype(NARROW)


def front_up_kernel(at, alive, mine, received, front, link, carried, solved):
    rows = pl.ds(at, carried.shape[0])
    operand = gather(0, mine[rows], received[rows], alive)
    result = (dot(operand, front[...], 1, 1) * alive[0:1, :]).astype(NARROW)
    solved[...] = result
    carried[...] = dot(result, link[...]).astype(NARROW)


def product_kernel(alive, front, link, fronts, links, downs, ups):
    across = alive[...].T
    for level in range(links.shape[0]):
        coupling = links[level]
        masked = (coupling.astype(WIDE) * across[:, level + 1 : level + 2]).astype(NARROW)
        ups[level] = dot(fronts[level], masked, 0, 0).astype(NARROW)
        downs[level + 1] = dot(fronts[level], coupling).astype(NARROW)
    downs[0] = dot(front[...], link[...]).astype(NARROW)


def front_pass_kernel(level, alive, mine, received, ups, carried, operand):
    value = gather(level, mine[...], received[...], alive)
    operand[...] = value
    carried[...] = dot(value, ups[level - 1]).astype(NARROW)


def front_solve_kernel(level, alive, operand, fronts, solved):
    solved[...] = (dot(operand[...], fronts[level - 1], 1, 1) * alive[level : level + 1, :]).astype(NARROW)


def top_kernel(levels, alive, mine, received, fronts, downs, *refs):
    *solved, back = refs
    operand = gather(levels - 1, mine[...], received[...], alive)
    current = (dot(operand, fronts[levels - 2], 1, 1) * alive[levels - 1 : levels, :]).astype(NARROW)
    for level in range(levels - 2, -1, -1):
        correction = dot(current, downs[level], 1, 1)
        value = solved[level][...].astype(WIDE) - correction
        current = (value * alive[level : level + 1, :]).astype(NARROW)
    back[...] = current


def lift_kernel(inverse, coupling, scale, lift):
    lift[...] = (dot(inverse[...], coupling[...]) * scale[0:1, 0:1]).astype(NARROW)


def down(first, spans, scale, lift, picked, half, out):
    size = out.shape[0]
    rows = pl.ds(0 if first else half.shape[0] - size, size)
    halves = jnp.concatenate([half[rows, pl.ds(at, width)] for at, width in spans], axis=1)
    result = halves.astype(WIDE) * scale[0:1, 0:1] - dot(lift[rows, :], picked, 1, 1)
    out[...] = result.astype(out.dtype)


def down_first_kernel(spans, rows, scale, lift, chosen, half, *refs):
    *backs, out, picked = refs
    back = jnp.concatenate([ref[pl.ds(at, width)] for ref, (at, width) in zip(backs, rows)], axis=0)
    values = dot(back, chosen[...]).astype(NARROW)
    picked[...] = values
    down(True, spans, scale, lift, values, half, out)


def down_second_kernel(spans, scale, lift, half, picked, out):
    down(False, spans, scale, lift, picked[...], half, out)


def add_kernel(kept, came, sent, rest):
    total = kept[...] + came[...].astype(WIDE)
    rows = sent.shape[0]
    sent[...] = total[:rows].astype(NARROW)
    rest[...] = total[rows:]


def last_add_kernel(kept, came, total):
    total[...] = kept[...] + came[...].astype(WIDE)


def body(
    leaf_rhs,
    leaf_inverse,
    leaf_coupling,
    leaf_rows,
    front_sizes,
    front_inverse,
    front_coupling,
    shift_weight,
):
    levels = lax.axis_size("leaf").bit_length() - 1
    shifts = lax.axis_size("shift")
    steps = shifts.bit_length() - 1
    core = lax.axis_index("leaf") & 1
    inverse_in, coupling_in, rhs_in = leaf_inverse[0, 0], leaf_coupling[0, 0], leaf_rhs[0]
    fronts_in, links_in = front_inverse[0, :, 0], front_coupling[0, :, 0]
    order, columns = rhs_in.shape
    front, boundary = fronts_in.shape[-1], coupling_in.shape[1]
    block = order // shifts
    unit = columns // (2 * sum(SHARES))
    widths = [share * unit for share in SHARES]
    offsets = [sum(widths[:n]) for n in range(len(widths))]
    def masks_of(step):
        if step == steps:
            return [0]
        stay = masks_of(step + 1)
        return [m | 1 << step for m in stay] + stay
    stay = masks_of(1)
    leave = [m | 1 for m in stay]

    chain = Chain()
    state = [dict() for _ in widths]
    final = [None for _ in widths]

    unknowns = jnp.arange(front, dtype=jnp.int32)[None, :]
    sizes = jnp.pad(front_sizes, (0, 8 - levels % 8))[:, None]
    held = {
        "alive": (unknowns < sizes).astype(WIDE),
        "scale": jnp.broadcast_to(shift_weight, (8, 128)).astype(WIDE),
    }

    unknowns = jnp.arange(front, dtype=jnp.int32)[None, :]
    sizes = jnp.pad(front_sizes, (0, 8 - levels % 8))[:, None]
    held = {
        "alive": (unknowns < sizes).astype(WIDE),
        "scale": jnp.broadcast_to(shift_weight, (8, 128)).astype(WIDE),
    }

    unknowns = jnp.arange(front, dtype=jnp.int32)[None, :]
    sizes = jnp.pad(front_sizes, (0, 8 - levels % 8))[:, None]
    held = {
        "alive": (unknowns < sizes).astype(WIDE),
        "scale": jnp.broadcast_to(shift_weight, (8, 128)).astype(WIDE),
    }

    def leaf(group):
        chunks = GROUPS[group]
        offset, width = offsets[chunks[0]], sum(widths[n] for n in chunks)
        outs = [((width, front), NARROW)] * 2 + [((order, 2 * width), NARROW)]
        if group == 0:
            shapes = [inverse_in.shape, coupling_in.shape, coupling_in.shape, rhs_in.shape, (front, front), (front, front)]
            names = ["chosen", "inverse", "mixed", "coupling", "rhs", "front", "link"]
            own, other, half, *loaded = chain(
                functools.partial(load_kernel, (*leave, *stay), width),
                [*outs, ((front, boundary), NARROW), *[(shape, NARROW) for shape in shapes]],
                [], [], "leaf_up",
                far=[rhs_in, inverse_in, coupling_in, leaf_rows, fronts_in, links_in],
                scratch=[
                    pltpu.VMEM(leaf_rows.shape, jnp.int32),
                    pltpu.SemaphoreType.DMA((10 + 2 * shifts,)),
                ],
            )
            held.update(zip(names, loaded))
        else:
            far = [fronts_in, links_in] if group == 1 else []
            outs += [((a.shape[0] - 1, front, front), NARROW) for a in far]
            own, other, half, *loaded = chain(
                functools.partial(leaf_up_kernel, offset, width), outs, [],
                [held[k] for k in ("inverse", "rhs", "mixed", "chosen")], "leaf_up",
                far=far, scratch=[pltpu.SemaphoreType.DMA((2,))] if far else [],
            )
            held.update(zip(("fronts", "links"), loaded))
        came = exchange(other, "leaf", 0)
        for n in chunks:
            at = offsets[n] - offset
            state[n].update(mine=own, came=came, half=half, solved=[], at=at, spans=(at, width + at))

    def up(n):
        width = widths[n]
        s = state[n]
        s["mine"], solved = chain(
            functools.partial(front_up_kernel, s["at"]), [((width, front), NARROW)] * 2, [],
            [held["alive"], s["mine"], s["came"], held["front"], held["link"]], "front_up",
        )
        s["solved"].append(solved)
        s["came"] = exchange(s["mine"], "leaf", 1)

    def products():
        held["downs"], held["ups"] = chain(
            product_kernel,
            [((levels - 1, front, front), NARROW), ((levels - 2, front, front), NARROW)],
            [], [held[k] for k in ("alive", "front", "link", "fronts", "links")], "products",
        )

    def middle(n):
        s = state[n]
        s["operands"] = []
        for level in range(1, levels - 1):
            s["mine"], operand = chain(
                functools.partial(front_pass_kernel, level), [((widths[n], front), NARROW)] * 2, [],
                [held["alive"], s["mine"], s["came"], held["ups"]], "front_pass",
            )
            s["operands"].append(operand)
            s["came"] = exchange(s["mine"], "leaf", level + 1)

    def solve(n):
        s = state[n]
        for level in range(1, levels - 1):
            s["solved"] += chain(
                functools.partial(front_solve_kernel, level), [((widths[n], front), NARROW)], [],
                [held["alive"], s["operands"][level - 1], held["fronts"]], "front_solve",
            )

    def top(n):
        s = state[n]
        (s["back"],) = chain(
            functools.partial(top_kernel, levels), [((widths[n], front), NARROW)], [],
            [held["alive"], s["mine"], s["came"], held["fronts"], held["downs"], *s["solved"]], "top",
        )
        s["back_came"] = exchange(s["back"], "leaf", 0)

    def lift():
        (held["lift"],) = chain(
            lift_kernel, [((order, boundary), NARROW)], [],
            [held["inverse"], held["coupling"], held["scale"]], "lift",
        )

    def pieces(n, part=0):
        spans = [(side, start * unit, width * unit) for side, start, width in PARTS[n][part]]
        return spans, sum(width for _, _, width in spans)

    def first(n, part=0):
        s = state[n]
        spans, width = pieces(n, part)
        inside = tuple((s["spans"][side] + start, size) for side, start, size in spans)
        sent, s["picked", part] = chain(
            functools.partial(down_first_kernel, inside, tuple(span[1:] for span in spans)),
            [((len(leave) * block, width), NARROW), ((width, boundary), NARROW)],
            [],
            [held["scale"], held["lift"], held["chosen"], s["half"], *[s["back_came" if side else "back"] for side, _, _ in spans]],
            "down_first",
        )
        s["sum_came", part] = exchange(sent, "shift", 0)

    def second(n, part=0):
        s = state[n]
        spans, width = pieces(n, part)
        inside = tuple((s["spans"][side] + start, size) for side, start, size in spans)
        (s["kept", part],) = chain(
            functools.partial(down_second_kernel, inside),
            [((len(stay) * block, width), WIDE)],
            [],
            [held["scale"], held["lift"], s["half"], s["picked", part]],
            "down_second",
        )

    def add(n, part=0):
        s = state[n]
        _, width = pieces(n, part)
        for step in range(1, steps):
            rows = block * (shifts >> step + 1)
            sent, s["kept", part] = chain(
                add_kernel, [((rows, width), NARROW), ((rows, width), WIDE)], [],
                [s["kept", part], s["sum_came", part]], "add",
            )
            s["sum_came", part] = exchange(sent, "shift", step)

    def last(n, part=0):
        s = state[n]
        (s["total", part],) = chain(
            last_add_kernel, [((block, pieces(n, part)[1]), WIDE)], [],
            [s["kept", part], s["sum_came", part]], "last_add",
        )

    run = {
        "A": leaf,
        "B": up,
        "C": middle,
        "T": solve,
        "Q": lambda n: products(),
        "D": top,
        "G": lambda n: lift(),
        "E": first,
        "S": second,
        "F": add,
        "Z": last,
    }
    for step in ORDER:
        chain.tag, _, cost = step.partition(":")
        chain.cost = float(cost or COST)
        run[step[0]](*[int(digit) for digit in chain.tag[1:] or "0"])

    sides = {}
    for n, chunk in enumerate(PARTS):
        for part in range(len(chunk)):
            at = 0
            for side, start, width in pieces(n, part)[0]:
                sides[side, offsets[n] + start] = state[n]["total", part][:, at : at + width]
                at += width
    owned = [sides[key] for key in sorted(sides) if not key[0]]
    others = [sides[key] for key in sorted(sides) if key[0]]
    low = jnp.concatenate(owned + others, axis=1)
    high = jnp.concatenate(others + owned, axis=1)
    return jnp.where(core == 0, low, high)[None]


ORDER = ("A0", "A1", "B0", "Q", "B1", "C0", "B2", "T0", "G", "C1", "T1", "D0", "E0", "C2", "T2", "D1", "S0", "F0", "E1", "D2", "E20", "Z0", "S20", "S1", "F1:3", "E21", "F20", "S21", "F21", "Z1", "Z20", "Z21")


def solution(mesh):
    in_specs = (
        P("leaf", None, None),
        P("shift", "leaf", None, None),
        P("shift", "leaf", None, None),
        P("leaf", None),
        P(),
        P("shift", None, "leaf", None, None),
        P("shift", None, "leaf", None, None),
        P("shift"),
    )
    out_specs = P("leaf", "shift", None)
    return jax.shard_map(body, mesh=mesh, in_specs=in_specs, out_specs=out_specs, check_vma=False)
```

```python
import functools

import jax
import jax.numpy as jnp
from jax import lax
from jax.experimental import pallas as pl
from jax.experimental.pallas import tpu as pltpu
from jax.sharding import PartitionSpec as P

WIDE = jnp.float32
NARROW = jnp.bfloat16
VMEM_LIMIT = 16 * 1024 * 1024
SHARES = (1, 1, 2)
GROUPS = ((0, 1), (2,))
PARTS = ((((0, 0, 1), (1, 0, 1)),), (((0, 0, 1), (1, 0, 1)),), (((0, 0, 2),), ((1, 0, 1),), ((1, 1, 1),)))
COST = 0.01
TILES = 2


def exchange(value, axis, bit):
    mask = 2**bit
    pairs = [(source, source ^ mask) for source in range(lax.axis_size(axis))]
    return lax.ppermute(value, axis, pairs)


def dot(left, right, left_dim=1, right_dim=0):
    return lax.dot_general(
        left, right, (((left_dim,), (right_dim,)), ((), ())), preferred_element_type=WIDE
    )


class Chain:
    def __init__(self):
        self.last = None
        self.tag = None
        self.cost = COST

    def __call__(self, kernel, outs, scalars, arrays, name, far=(), spaces=None, scratch=(), place=None):
        after = [] if self.last is None else [self.last]
        spaces = spaces or [pltpu.VMEM] * len(outs)
        taken = [] if place is None else [place]
        aliases = {len(after) + len(scalars) + len(arrays): 0} if taken else {}

        def run(*refs):
            kernel(*refs[len(after) :])

        results = pl.pallas_call(
            run,
            out_shape=[jax.ShapeDtypeStruct(shape, kind) for shape, kind in outs],
            in_specs=[pl.BlockSpec(memory_space=pl.ANY)] * len(after)
            + [pl.BlockSpec(memory_space=pltpu.SMEM)] * len(scalars)
            + [pl.BlockSpec(memory_space=pltpu.VMEM)] * len(arrays)
            + [pl.BlockSpec(memory_space=pltpu.HBM)] * len(taken)
            + [pl.BlockSpec(memory_space=pl.ANY)] * len(far),
            out_specs=[pl.BlockSpec(memory_space=space) for space in spaces],
            input_output_aliases=aliases,
            scratch_shapes=scratch,
            cost_estimate=pl.CostEstimate(
                flops=int(self.cost * 1.15e9), bytes_accessed=1, transcendentals=0
            ),
            compiler_params=pltpu.CompilerParams(vmem_limit_bytes=VMEM_LIMIT),
            name=self.tag + "_" + name,
        )(*after, *scalars, *arrays, *taken, *[pltpu.with_memory_space_constraint(a, pltpu.HBM) for a in far])
        self.last = results[-1]
        return results


def selector(rows, front):
    at = lax.broadcasted_iota(jnp.int32, (front, rows.shape[1]), 0)
    return (at == rows[...]).astype(WIDE).astype(NARROW)


def load_kernel(masks, width, rhs_in, inverse_in, coupling_in, rows_in, fronts_in, links_in, *refs):
    own, other, half, chosen, inverse, mixed, coupling, rhs, front, link, rows, sems = refs
    count = rhs.shape[1] // 2
    block = inverse.shape[0] // len(masks)
    core = lax.axis_index("leaf") & 1
    shift = lax.axis_index("shift")
    copies = []

    def load(source, target):
        copies.append(pltpu.make_async_copy(source, target, sems.at[len(copies)]))
        copies[-1].start()
        return copies[-1]

    def load_columns(start, size):
        return [
            load(
                rhs_in.at[:, pl.ds(pl.multiple_of(side * count + start, 128), size)],
                rhs.at[:, pl.ds(number * count + start, size)],
            )
            for number, side in enumerate((core, 1 - core))
        ]

    def load_blocks(source, target):
        return [
            load(
                source.at[pl.ds(pl.multiple_of((shift ^ mask) * block, block), block)],
                target.at[pl.ds(number * block, block)],
            )
            for number, mask in enumerate(masks)
        ]

    first = load_columns(0, width)
    blocks = load_blocks(inverse_in, inverse)
    small = [load(rows_in, rows)]
    small += load_blocks(coupling_in, mixed)

    for copy in first:
        copy.wait()
    both = jnp.concatenate([rhs[:, :width], rhs[:, count : count + width]], axis=1)
    parts = TILES
    for part in range(parts):
        for copy in blocks[part * len(blocks) // parts : (part + 1) * len(blocks) // parts]:
            copy.wait()
        if part == parts - 1:
            later = [load(fronts_in.at[0], front), load(links_in.at[0], link), load(coupling_in, coupling)]
            if width < count:
                later += load_columns(width, count - width)
        tile = pl.ds(part * (inverse.shape[0] // parts), inverse.shape[0] // parts)
        half[tile, :] = dot(inverse[tile, :], both).astype(NARROW)
    for copy in small:
        copy.wait()
    selected = selector(rows, own.shape[1])
    chosen[...] = selected
    boundary = dot(half[...], mixed[...], 0, 0).astype(NARROW)
    placed = dot(boundary, selected, 1, 1).astype(NARROW)
    own[...] = placed[:width]
    other[...] = placed[width:]
    for copy in later:
        copy.wait()


def leaf_up_kernel(offset, width, inverse, rhs, mixed, chosen, *refs):
    if len(refs) > 3:
        fronts_in, links_in, own, other, half, fronts, links, sems = refs
        copies = [
            pltpu.make_async_copy(source.at[pl.ds(1, target.shape[0])], target, sems.at[number])
            for number, (source, target) in enumerate(((fronts_in, fronts), (links_in, links)))
        ]
    else:
        own, other, half = refs
        copies = []
    for copy in copies:
        copy.start()
    count = rhs.shape[1] // 2
    both = jnp.concatenate(
        [rhs[:, offset : offset + width], rhs[:, count + offset : count + offset + width]], axis=1
    )
    product = dot(inverse[...], both).astype(NARROW)
    half[...] = product
    boundary = dot(product, mixed[...], 0, 0).astype(NARROW)
    placed = dot(boundary, chosen[...], 1, 1).astype(NARROW)
    own[...] = placed[:width]
    other[...] = placed[width:]
    for copy in copies:
        copy.wait()


def gather(level, mine, received, alive):
    total = mine.astype(WIDE) + received.astype(WIDE)
    return (total * alive[level : level + 1, :]).astype(NARROW)


def front_up_kernel(at, alive, mine, received, front, link, carried, solved):
    rows = pl.ds(at, carried.shape[0])
    operand = gather(0, mine[rows], received[rows], alive)
    result = (dot(operand, front[...], 1, 1) * alive[0:1, :]).astype(NARROW)
    solved[...] = result
    carried[...] = dot(result, link[...]).astype(NARROW)


def product_kernel(alive, front, link, fronts, links, downs, ups):
    across = alive[...].T
    for level in range(links.shape[0]):
        coupling = links[level]
        masked = (coupling.astype(WIDE) * across[:, level + 1 : level + 2]).astype(NARROW)
        ups[level] = dot(fronts[level], masked, 0, 0).astype(NARROW)
        downs[level + 1] = dot(fronts[level], coupling).astype(NARROW)
    downs[0] = dot(front[...], link[...]).astype(NARROW)


def front_pass_kernel(level, alive, mine, received, ups, carried, operand):
    value = gather(level, mine[...], received[...], alive)
    operand[...] = value
    carried[...] = dot(value, ups[level - 1]).astype(NARROW)


def front_solve_kernel(level, alive, operand, fronts, solved):
    solved[...] = (dot(operand[...], fronts[level - 1], 1, 1) * alive[level : level + 1, :]).astype(NARROW)


def top_kernel(levels, alive, mine, received, fronts, downs, *refs):
    *solved, back = refs
    operand = gather(levels - 1, mine[...], received[...], alive)
    current = (dot(operand, fronts[levels - 2], 1, 1) * alive[levels - 1 : levels, :]).astype(NARROW)
    for level in range(levels - 2, -1, -1):
        correction = dot(current, downs[level], 1, 1)
        value = solved[level][...].astype(WIDE) - correction
        current = (value * alive[level : level + 1, :]).astype(NARROW)
    back[...] = current


def lift_kernel(inverse, coupling, scale, lift):
    lift[...] = (dot(inverse[...], coupling[...]) * scale[0:1, 0:1]).astype(NARROW)


def down(first, spans, scale, lift, picked, half, out):
    size = out.shape[0]
    rows = pl.ds(0 if first else half.shape[0] - size, size)
    halves = jnp.concatenate([half[rows, pl.ds(at, width)] for at, width in spans], axis=1)
    result = halves.astype(WIDE) * scale[0:1, 0:1] - dot(lift[rows, :], picked, 1, 1)
    out[...] = result.astype(out.dtype)


def down_first_kernel(spans, rows, scale, lift, chosen, half, *refs):
    *backs, out, picked = refs
    back = jnp.concatenate([ref[pl.ds(at, width)] for ref, (at, width) in zip(backs, rows)], axis=0)
    values = dot(back, chosen[...]).astype(NARROW)
    picked[...] = values
    down(True, spans, scale, lift, values, half, out)


def down_second_kernel(spans, scale, lift, half, picked, out):
    down(False, spans, scale, lift, picked[...], half, out)


def add_kernel(kept, came, sent, rest):
    total = kept[...] + came[...].astype(WIDE)
    rows = sent.shape[0]
    sent[...] = total[:rows].astype(NARROW)
    rest[...] = total[rows:]


def finish_kernel(spans, kept, came, *refs):
    out, token, total, sems = refs[-4:]
    count = out.shape[1] // 2
    core = lax.axis_index("leaf") & 1
    total[...] = kept[...] + came[...].astype(WIDE)
    token[...] = jnp.zeros_like(token)
    copies, at = [], 0
    for number, (side, start, width) in enumerate(spans):
        column = (core if side == 0 else 1 - core) * count + start
        target = out.at[:, pl.ds(pl.multiple_of(column, 128), width)]
        copies.append(pltpu.make_async_copy(total.at[:, pl.ds(at, width)], target, sems.at[number]))
        copies[-1].start()
        at += width
    for copy in copies:
        copy.wait()


def body(
    leaf_rhs,
    leaf_inverse,
    leaf_coupling,
    leaf_rows,
    front_sizes,
    front_inverse,
    front_coupling,
    shift_weight,
):
    levels = lax.axis_size("leaf").bit_length() - 1
    shifts = lax.axis_size("shift")
    steps = shifts.bit_length() - 1
    inverse_in, coupling_in, rhs_in = leaf_inverse[0, 0], leaf_coupling[0, 0], leaf_rhs[0]
    fronts_in, links_in = front_inverse[0, :, 0], front_coupling[0, :, 0]
    order, columns = rhs_in.shape
    front, boundary = fronts_in.shape[-1], coupling_in.shape[1]
    block = order // shifts
    unit = columns // (2 * sum(SHARES))
    widths = [share * unit for share in SHARES]
    offsets = [sum(widths[:n]) for n in range(len(widths))]
    def masks_of(step):
        if step == steps:
            return [0]
        stay = masks_of(step + 1)
        return [m | 1 << step for m in stay] + stay
    stay = masks_of(1)
    leave = [m | 1 for m in stay]

    chain = Chain()
    state = [dict() for _ in widths]
    final = [None for _ in widths]

    unknowns = jnp.arange(front, dtype=jnp.int32)[None, :]
    sizes = jnp.pad(front_sizes, (0, 8 - levels % 8))[:, None]
    held = {
        "alive": (unknowns < sizes).astype(WIDE),
        "scale": jnp.broadcast_to(shift_weight, (8, 128)).astype(WIDE),
    }

    unknowns = jnp.arange(front, dtype=jnp.int32)[None, :]
    sizes = jnp.pad(front_sizes, (0, 8 - levels % 8))[:, None]
    held = {
        "alive": (unknowns < sizes).astype(WIDE),
        "scale": jnp.broadcast_to(shift_weight, (8, 128)).astype(WIDE),
    }

    unknowns = jnp.arange(front, dtype=jnp.int32)[None, :]
    sizes = jnp.pad(front_sizes, (0, 8 - levels % 8))[:, None]
    held = {
        "alive": (unknowns < sizes).astype(WIDE),
        "scale": jnp.broadcast_to(shift_weight, (8, 128)).astype(WIDE),
    }

    def leaf(group):
        chunks = GROUPS[group]
        offset, width = offsets[chunks[0]], sum(widths[n] for n in chunks)
        outs = [((width, front), NARROW)] * 2 + [((order, 2 * width), NARROW)]
        if group == 0:
            shapes = [inverse_in.shape, coupling_in.shape, coupling_in.shape, rhs_in.shape, (front, front), (front, front)]
            names = ["chosen", "inverse", "mixed", "coupling", "rhs", "front", "link"]
            own, other, half, *loaded = chain(
                functools.partial(load_kernel, (*leave, *stay), width),
                [*outs, ((front, boundary), NARROW), *[(shape, NARROW) for shape in shapes]],
                [], [], "leaf_up",
                far=[rhs_in, inverse_in, coupling_in, leaf_rows, fronts_in, links_in],
                scratch=[
                    pltpu.VMEM(leaf_rows.shape, jnp.int32),
                    pltpu.SemaphoreType.DMA((10 + 2 * shifts,)),
                ],
            )
            held.update(zip(names, loaded))
        else:
            far = [fronts_in, links_in] if group == 1 else []
            outs += [((a.shape[0] - 1, front, front), NARROW) for a in far]
            own, other, half, *loaded = chain(
                functools.partial(leaf_up_kernel, offset, width), outs, [],
                [held[k] for k in ("inverse", "rhs", "mixed", "chosen")], "leaf_up",
                far=far, scratch=[pltpu.SemaphoreType.DMA((2,))] if far else [],
            )
            held.update(zip(("fronts", "links"), loaded))
        came = exchange(other, "leaf", 0)
        for n in chunks:
            at = offsets[n] - offset
            state[n].update(mine=own, came=came, half=half, solved=[], at=at, spans=(at, width + at))

    def up(n):
        width = widths[n]
        s = state[n]
        s["mine"], solved = chain(
            functools.partial(front_up_kernel, s["at"]), [((width, front), NARROW)] * 2, [],
            [held["alive"], s["mine"], s["came"], held["front"], held["link"]], "front_up",
        )
        s["solved"].append(solved)
        s["came"] = exchange(s["mine"], "leaf", 1)

    def products():
        held["downs"], held["ups"] = chain(
            product_kernel,
            [((levels - 1, front, front), NARROW), ((levels - 2, front, front), NARROW)],
            [], [held[k] for k in ("alive", "front", "link", "fronts", "links")], "products",
        )

    def middle(n):
        s = state[n]
        s["operands"] = []
        for level in range(1, levels - 1):
            s["mine"], operand = chain(
                functools.partial(front_pass_kernel, level), [((widths[n], front), NARROW)] * 2, [],
                [held["alive"], s["mine"], s["came"], held["ups"]], "front_pass",
            )
            s["operands"].append(operand)
            s["came"] = exchange(s["mine"], "leaf", level + 1)

    def solve(n):
        s = state[n]
        for level in range(1, levels - 1):
            s["solved"] += chain(
                functools.partial(front_solve_kernel, level), [((widths[n], front), NARROW)], [],
                [held["alive"], s["operands"][level - 1], held["fronts"]], "front_solve",
            )

    def top(n):
        s = state[n]
        (s["back"],) = chain(
            functools.partial(top_kernel, levels), [((widths[n], front), NARROW)], [],
            [held["alive"], s["mine"], s["came"], held["fronts"], held["downs"], *s["solved"]], "top",
        )
        s["back_came"] = exchange(s["back"], "leaf", 0)

    def lift():
        (held["lift"],) = chain(
            lift_kernel, [((order, boundary), NARROW)], [],
            [held["inverse"], held["coupling"], held["scale"]], "lift",
        )

    def pieces(n, part=0):
        spans = [(side, start * unit, width * unit) for side, start, width in PARTS[n][part]]
        return spans, sum(width for _, _, width in spans)

    def first(n, part=0):
        s = state[n]
        spans, width = pieces(n, part)
        inside = tuple((s["spans"][side] + start, size) for side, start, size in spans)
        sent, s["picked", part] = chain(
            functools.partial(down_first_kernel, inside, tuple(span[1:] for span in spans)),
            [((len(leave) * block, width), NARROW), ((width, boundary), NARROW)],
            [],
            [held["scale"], held["lift"], held["chosen"], s["half"], *[s["back_came" if side else "back"] for side, _, _ in spans]],
            "down_first",
        )
        s["sum_came", part] = exchange(sent, "shift", 0)

    def second(n, part=0):
        s = state[n]
        spans, width = pieces(n, part)
        inside = tuple((s["spans"][side] + start, size) for side, start, size in spans)
        (s["kept", part],) = chain(
            functools.partial(down_second_kernel, inside),
            [((len(stay) * block, width), WIDE)],
            [],
            [held["scale"], held["lift"], s["half"], s["picked", part]],
            "down_second",
        )

    def add(n, part=0):
        s = state[n]
        _, width = pieces(n, part)
        for step in range(1, steps):
            rows = block * (shifts >> step + 1)
            sent, s["kept", part] = chain(
                add_kernel, [((rows, width), NARROW), ((rows, width), WIDE)], [],
                [s["kept", part], s["sum_came", part]], "add",
            )
            s["sum_came", part] = exchange(sent, "shift", step)

    def last(n, part=0):
        s = state[n]
        spans, width = pieces(n, part)
        targets = tuple((side, offsets[n] + start, size) for side, start, size in spans)
        held["out"], _ = chain(
            functools.partial(finish_kernel, targets), [((block, columns), WIDE), ((8, 128), WIDE)], [],
            [s["kept", part], s["sum_came", part]], "finish", place=held.get("out"),
            spaces=[pltpu.HBM, pltpu.VMEM],
            scratch=[pltpu.VMEM((block, width), WIDE), pltpu.SemaphoreType.DMA((len(spans),))],
        )

    run = {
        "A": leaf,
        "B": up,
        "C": middle,
        "T": solve,
        "Q": lambda n: products(),
        "D": top,
        "G": lambda n: lift(),
        "E": first,
        "S": second,
        "F": add,
        "Z": last,
    }
    for step in ORDER:
        chain.tag, _, cost = step.partition(":")
        chain.cost = float(cost or COST)
        run[step[0]](*[int(digit) for digit in chain.tag[1:] or "0"])

    return held["out"][None]


ORDER = ("A0", "A1", "B0:0.5", "Q", "B1", "C0:0.5", "B2", "G", "C1", "T1", "T0", "D0", "E0", "C2", "S0", "D1", "F0:0.5", "E1", "T2", "D2", "E20", "S1", "F1", "Z0:3", "E21", "S20", "S21", "E22", "F20", "S22", "Z1", "F21", "F22", "Z20", "Z21", "Z22:0.5")


def solution(mesh):
    in_specs = (
        P("leaf", None, None),
        P("shift", "leaf", None, None),
        P("shift", "leaf", None, None),
        P("leaf", None),
        P(),
        P("shift", None, "leaf", None, None),
        P("shift", None, "leaf", None, None),
        P("shift"),
    )
    out_specs = P("leaf", "shift", None)
    return jax.shard_map(body, mesh=mesh, in_specs=in_specs, out_specs=out_specs, check_vma=False)
```

```python
import functools

import jax
import jax.numpy as jnp
from jax import lax
from jax.experimental import pallas as pl
from jax.experimental.pallas import tpu as pltpu
from jax.sharding import PartitionSpec as P

WIDE = jnp.float32
NARROW = jnp.bfloat16
VMEM_LIMIT = 16 * 1024 * 1024
SHARES = (1, 1, 2)
GROUPS = ((0, 1), (2,))
PARTS = ((((0, 0, 1), (1, 0, 1)),), (((0, 0, 1), (1, 0, 1)),), (((0, 0, 2),), ((1, 0, 1),), ((1, 1, 1),)))
COST = 0.01
TILES = 4


def exchange(value, axis, bit):
    mask = 2**bit
    pairs = [(source, source ^ mask) for source in range(lax.axis_size(axis))]
    return lax.ppermute(value, axis, pairs)


def dot(left, right, left_dim=1, right_dim=0):
    return lax.dot_general(
        left, right, (((left_dim,), (right_dim,)), ((), ())), preferred_element_type=WIDE
    )


class Chain:
    def __init__(self):
        self.last = None
        self.tag = None
        self.cost = COST

    def __call__(self, kernel, outs, scalars, arrays, name, far=(), spaces=None, scratch=(), place=None):
        after = [] if self.last is None else [self.last]
        spaces = spaces or [pltpu.VMEM] * len(outs)
        taken = [] if place is None else [place]
        aliases = {len(after) + len(scalars) + len(arrays): 0} if taken else {}

        def run(*refs):
            kernel(*refs[len(after) :])

        results = pl.pallas_call(
            run,
            out_shape=[jax.ShapeDtypeStruct(shape, kind) for shape, kind in outs],
            in_specs=[pl.BlockSpec(memory_space=pl.ANY)] * len(after)
            + [pl.BlockSpec(memory_space=pltpu.SMEM)] * len(scalars)
            + [pl.BlockSpec(memory_space=pltpu.VMEM)] * len(arrays)
            + [pl.BlockSpec(memory_space=pltpu.HBM)] * len(taken)
            + [pl.BlockSpec(memory_space=pl.ANY)] * len(far),
            out_specs=[pl.BlockSpec(memory_space=space) for space in spaces],
            input_output_aliases=aliases,
            scratch_shapes=scratch,
            cost_estimate=pl.CostEstimate(
                flops=int(self.cost * 1.15e9), bytes_accessed=1, transcendentals=0
            ),
            compiler_params=pltpu.CompilerParams(vmem_limit_bytes=VMEM_LIMIT),
            name=self.tag + "_" + name,
        )(*after, *scalars, *arrays, *taken, *[pltpu.with_memory_space_constraint(a, pltpu.HBM) for a in far])
        self.last = results[-1]
        return results


def selector(rows, front):
    at = lax.broadcasted_iota(jnp.int32, (front, rows.shape[1]), 0)
    return (at == rows[...]).astype(WIDE).astype(NARROW)


def load_kernel(masks, width, rhs_in, inverse_in, coupling_in, rows_in, fronts_in, links_in, *refs):
    own, other, half, chosen, inverse, mixed, coupling, rhs, front, link, rows, sems = refs
    count = rhs.shape[1] // 2
    block = inverse.shape[0] // len(masks)
    core = lax.axis_index("leaf") & 1
    shift = lax.axis_index("shift")
    copies = []

    def load(source, target):
        copies.append(pltpu.make_async_copy(source, target, sems.at[len(copies)]))
        copies[-1].start()
        return copies[-1]

    def load_columns(start, size):
        return [
            load(
                rhs_in.at[:, pl.ds(pl.multiple_of(side * count + start, 128), size)],
                rhs.at[:, pl.ds(number * count + start, size)],
            )
            for number, side in enumerate((core, 1 - core))
        ]

    def load_blocks(source, target):
        return [
            load(
                source.at[pl.ds(pl.multiple_of((shift ^ mask) * block, block), block)],
                target.at[pl.ds(number * block, block)],
            )
            for number, mask in enumerate(masks)
        ]

    first = load_columns(0, width)
    blocks = load_blocks(inverse_in, inverse)
    small = [load(rows_in, rows)]
    small += load_blocks(coupling_in, mixed)

    for copy in first:
        copy.wait()
    both = jnp.concatenate([rhs[:, :width], rhs[:, count : count + width]], axis=1)
    parts = TILES
    for part in range(parts):
        for copy in blocks[part * len(blocks) // parts : (part + 1) * len(blocks) // parts]:
            copy.wait()
        if part == 0:
            later = [load(fronts_in.at[0], front), load(links_in.at[0], link), load(coupling_in, coupling)]
            if width < count:
                later += load_columns(width, count - width)
        tile = pl.ds(part * (inverse.shape[0] // parts), inverse.shape[0] // parts)
        half[tile, :] = dot(inverse[tile, :], both).astype(NARROW)
    for copy in small:
        copy.wait()
    selected = selector(rows, own.shape[1])
    chosen[...] = selected
    boundary = dot(half[...], mixed[...], 0, 0).astype(NARROW)
    placed = dot(boundary, selected, 1, 1).astype(NARROW)
    own[...] = placed[:width]
    other[...] = placed[width:]
    for copy in later:
        copy.wait()


def leaf_up_kernel(offset, width, inverse, rhs, mixed, chosen, *refs):
    if len(refs) > 3:
        fronts_in, links_in, own, other, half, fronts, links, sems = refs
        copies = [
            pltpu.make_async_copy(source.at[pl.ds(1, target.shape[0])], target, sems.at[number])
            for number, (source, target) in enumerate(((fronts_in, fronts), (links_in, links)))
        ]
    else:
        own, other, half = refs
        copies = []
    for copy in copies:
        copy.start()
    count = rhs.shape[1] // 2
    both = jnp.concatenate(
        [rhs[:, offset : offset + width], rhs[:, count + offset : count + offset + width]], axis=1
    )
    product = dot(inverse[...], both).astype(NARROW)
    half[...] = product
    boundary = dot(product, mixed[...], 0, 0).astype(NARROW)
    placed = dot(boundary, chosen[...], 1, 1).astype(NARROW)
    own[...] = placed[:width]
    other[...] = placed[width:]
    for copy in copies:
        copy.wait()


def gather(level, mine, received, alive):
    total = mine.astype(WIDE) + received.astype(WIDE)
    return (total * alive[level : level + 1, :]).astype(NARROW)


def front_up_kernel(at, alive, mine, received, front, link, carried, solved):
    rows = pl.ds(at, carried.shape[0])
    operand = gather(0, mine[rows], received[rows], alive)
    result = (dot(operand, front[...], 1, 1) * alive[0:1, :]).astype(NARROW)
    solved[...] = result
    carried[...] = dot(result, link[...]).astype(NARROW)


def product_kernel(alive, front, link, fronts, links, downs, ups):
    across = alive[...].T
    for level in range(links.shape[0]):
        coupling = links[level]
        masked = (coupling.astype(WIDE) * across[:, level + 1 : level + 2]).astype(NARROW)
        ups[level] = dot(fronts[level], masked, 0, 0).astype(NARROW)
        downs[level + 1] = dot(fronts[level], coupling).astype(NARROW)
    downs[0] = dot(front[...], link[...]).astype(NARROW)


def front_pass_kernel(level, alive, mine, received, ups, carried, operand):
    value = gather(level, mine[...], received[...], alive)
    operand[...] = value
    carried[...] = dot(value, ups[level - 1]).astype(NARROW)


def front_solve_kernel(level, alive, operand, fronts, solved):
    solved[...] = (dot(operand[...], fronts[level - 1], 1, 1) * alive[level : level + 1, :]).astype(NARROW)


def top_kernel(levels, alive, mine, received, fronts, downs, *refs):
    *solved, back = refs
    operand = gather(levels - 1, mine[...], received[...], alive)
    current = (dot(operand, fronts[levels - 2], 1, 1) * alive[levels - 1 : levels, :]).astype(NARROW)
    for level in range(levels - 2, -1, -1):
        correction = dot(current, downs[level], 1, 1)
        value = solved[level][...].astype(WIDE) - correction
        current = (value * alive[level : level + 1, :]).astype(NARROW)
    back[...] = current


def lift_kernel(inverse, coupling, scale, lift):
    lift[...] = (dot(inverse[...], coupling[...]) * scale[0:1, 0:1]).astype(NARROW)


def down(first, spans, scale, lift, picked, half, out):
    size = out.shape[0]
    rows = pl.ds(0 if first else half.shape[0] - size, size)
    halves = jnp.concatenate([half[rows, pl.ds(at, width)] for at, width in spans], axis=1)
    result = halves.astype(WIDE) * scale[0:1, 0:1] - dot(lift[rows, :], picked, 1, 1)
    out[...] = result.astype(out.dtype)


def down_first_kernel(spans, rows, scale, lift, chosen, half, *refs):
    *backs, out, picked = refs
    back = jnp.concatenate([ref[pl.ds(at, width)] for ref, (at, width) in zip(backs, rows)], axis=0)
    values = dot(back, chosen[...]).astype(NARROW)
    picked[...] = values
    down(True, spans, scale, lift, values, half, out)


def down_second_kernel(spans, scale, lift, half, picked, out):
    down(False, spans, scale, lift, picked[...], half, out)


def add_kernel(kept, came, sent, rest):
    total = kept[...] + came[...].astype(WIDE)
    rows = sent.shape[0]
    sent[...] = total[:rows].astype(NARROW)
    rest[...] = total[rows:]


def finish_kernel(spans, kept, came, *refs):
    out, token, total, sems = refs[-4:]
    count = out.shape[1] // 2
    core = lax.axis_index("leaf") & 1
    total[...] = kept[...] + came[...].astype(WIDE)
    token[...] = jnp.zeros_like(token)
    copies, at = [], 0
    for number, (side, start, width) in enumerate(spans):
        column = (core if side == 0 else 1 - core) * count + start
        target = out.at[:, pl.ds(pl.multiple_of(column, 128), width)]
        copies.append(pltpu.make_async_copy(total.at[:, pl.ds(at, width)], target, sems.at[number]))
        copies[-1].start()
        at += width
    for copy in copies:
        copy.wait()


def body(
    leaf_rhs,
    leaf_inverse,
    leaf_coupling,
    leaf_rows,
    front_sizes,
    front_inverse,
    front_coupling,
    shift_weight,
):
    levels = lax.axis_size("leaf").bit_length() - 1
    shifts = lax.axis_size("shift")
    steps = shifts.bit_length() - 1
    inverse_in, coupling_in, rhs_in = leaf_inverse[0, 0], leaf_coupling[0, 0], leaf_rhs[0]
    fronts_in, links_in = front_inverse[0, :, 0], front_coupling[0, :, 0]
    order, columns = rhs_in.shape
    front, boundary = fronts_in.shape[-1], coupling_in.shape[1]
    block = order // shifts
    unit = columns // (2 * sum(SHARES))
    widths = [share * unit for share in SHARES]
    offsets = [sum(widths[:n]) for n in range(len(widths))]
    def masks_of(step):
        if step == steps:
            return [0]
        stay = masks_of(step + 1)
        return [m | 1 << step for m in stay] + stay
    stay = masks_of(1)
    leave = [m | 1 for m in stay]

    chain = Chain()
    state = [dict() for _ in widths]
    final = [None for _ in widths]

    unknowns = jnp.arange(front, dtype=jnp.int32)[None, :]
    sizes = jnp.pad(front_sizes, (0, 8 - levels % 8))[:, None]
    held = {
        "alive": (unknowns < sizes).astype(WIDE),
        "scale": jnp.broadcast_to(shift_weight, (8, 128)).astype(WIDE),
    }

    unknowns = jnp.arange(front, dtype=jnp.int32)[None, :]
    sizes = jnp.pad(front_sizes, (0, 8 - levels % 8))[:, None]
    held = {
        "alive": (unknowns < sizes).astype(WIDE),
        "scale": jnp.broadcast_to(shift_weight, (8, 128)).astype(WIDE),
    }

    unknowns = jnp.arange(front, dtype=jnp.int32)[None, :]
    sizes = jnp.pad(front_sizes, (0, 8 - levels % 8))[:, None]
    held = {
        "alive": (unknowns < sizes).astype(WIDE),
        "scale": jnp.broadcast_to(shift_weight, (8, 128)).astype(WIDE),
    }

    def leaf(group):
        chunks = GROUPS[group]
        offset, width = offsets[chunks[0]], sum(widths[n] for n in chunks)
        outs = [((width, front), NARROW)] * 2 + [((order, 2 * width), NARROW)]
        if group == 0:
            shapes = [inverse_in.shape, coupling_in.shape, coupling_in.shape, rhs_in.shape, (front, front), (front, front)]
            names = ["chosen", "inverse", "mixed", "coupling", "rhs", "front", "link"]
            own, other, half, *loaded = chain(
                functools.partial(load_kernel, (*leave, *stay), width),
                [*outs, ((front, boundary), NARROW), *[(shape, NARROW) for shape in shapes]],
                [], [], "leaf_up",
                far=[rhs_in, inverse_in, coupling_in, leaf_rows, fronts_in, links_in],
                scratch=[
                    pltpu.VMEM(leaf_rows.shape, jnp.int32),
                    pltpu.SemaphoreType.DMA((10 + 2 * shifts,)),
                ],
            )
            held.update(zip(names, loaded))
        else:
            far = [fronts_in, links_in] if group == 1 else []
            outs += [((a.shape[0] - 1, front, front), NARROW) for a in far]
            own, other, half, *loaded = chain(
                functools.partial(leaf_up_kernel, offset, width), outs, [],
                [held[k] for k in ("inverse", "rhs", "mixed", "chosen")], "leaf_up",
                far=far, scratch=[pltpu.SemaphoreType.DMA((2,))] if far else [],
            )
            held.update(zip(("fronts", "links"), loaded))
        came = exchange(other, "leaf", 0)
        for n in chunks:
            at = offsets[n] - offset
            state[n].update(mine=own, came=came, half=half, solved=[], at=at, spans=(at, width + at))

    def up(n):
        width = widths[n]
        s = state[n]
        s["mine"], solved = chain(
            functools.partial(front_up_kernel, s["at"]), [((width, front), NARROW)] * 2, [],
            [held["alive"], s["mine"], s["came"], held["front"], held["link"]], "front_up",
        )
        s["solved"].append(solved)
        s["came"] = exchange(s["mine"], "leaf", 1)

    def products():
        held["downs"], held["ups"] = chain(
            product_kernel,
            [((levels - 1, front, front), NARROW), ((levels - 2, front, front), NARROW)],
            [], [held[k] for k in ("alive", "front", "link", "fronts", "links")], "products",
        )

    def middle(n):
        s = state[n]
        s["operands"] = []
        for level in range(1, levels - 1):
            s["mine"], operand = chain(
                functools.partial(front_pass_kernel, level), [((widths[n], front), NARROW)] * 2, [],
                [held["alive"], s["mine"], s["came"], held["ups"]], "front_pass",
            )
            s["operands"].append(operand)
            s["came"] = exchange(s["mine"], "leaf", level + 1)

    def solve(n):
        s = state[n]
        for level in range(1, levels - 1):
            s["solved"] += chain(
                functools.partial(front_solve_kernel, level), [((widths[n], front), NARROW)], [],
                [held["alive"], s["operands"][level - 1], held["fronts"]], "front_solve",
            )

    def top(n):
        s = state[n]
        (s["back"],) = chain(
            functools.partial(top_kernel, levels), [((widths[n], front), NARROW)], [],
            [held["alive"], s["mine"], s["came"], held["fronts"], held["downs"], *s["solved"]], "top",
        )
        s["back_came"] = exchange(s["back"], "leaf", 0)

    def lift():
        (held["lift"],) = chain(
            lift_kernel, [((order, boundary), NARROW)], [],
            [held["inverse"], held["coupling"], held["scale"]], "lift",
        )

    def pieces(n, part=0):
        spans = [(side, start * unit, width * unit) for side, start, width in PARTS[n][part]]
        return spans, sum(width for _, _, width in spans)

    def first(n, part=0):
        s = state[n]
        spans, width = pieces(n, part)
        inside = tuple((s["spans"][side] + start, size) for side, start, size in spans)
        sent, s["picked", part] = chain(
            functools.partial(down_first_kernel, inside, tuple(span[1:] for span in spans)),
            [((len(leave) * block, width), NARROW), ((width, boundary), NARROW)],
            [],
            [held["scale"], held["lift"], held["chosen"], s["half"], *[s["back_came" if side else "back"] for side, _, _ in spans]],
            "down_first",
        )
        s["sum_came", part] = exchange(sent, "shift", 0)

    def second(n, part=0):
        s = state[n]
        spans, width = pieces(n, part)
        inside = tuple((s["spans"][side] + start, size) for side, start, size in spans)
        (s["kept", part],) = chain(
            functools.partial(down_second_kernel, inside),
            [((len(stay) * block, width), WIDE)],
            [],
            [held["scale"], held["lift"], s["half"], s["picked", part]],
            "down_second",
        )

    def add(n, part=0):
        s = state[n]
        _, width = pieces(n, part)
        for step in range(1, steps):
            rows = block * (shifts >> step + 1)
            sent, s["kept", part] = chain(
                add_kernel, [((rows, width), NARROW), ((rows, width), WIDE)], [],
                [s["kept", part], s["sum_came", part]], "add",
            )
            s["sum_came", part] = exchange(sent, "shift", step)

    def last(n, part=0):
        s = state[n]
        spans, width = pieces(n, part)
        targets = tuple((side, offsets[n] + start, size) for side, start, size in spans)
        held["out"], _ = chain(
            functools.partial(finish_kernel, targets), [((block, columns), WIDE), ((8, 128), WIDE)], [],
            [s["kept", part], s["sum_came", part]], "finish", place=held.get("out"),
            spaces=[pltpu.HBM, pltpu.VMEM],
            scratch=[pltpu.VMEM((block, width), WIDE), pltpu.SemaphoreType.DMA((len(spans),))],
        )

    run = {
        "A": leaf,
        "B": up,
        "C": middle,
        "T": solve,
        "Q": lambda n: products(),
        "D": top,
        "G": lambda n: lift(),
        "E": first,
        "S": second,
        "F": add,
        "Z": last,
    }
    for step in ORDER:
        chain.tag, _, cost = step.partition(":")
        chain.cost = float(cost or COST)
        run[step[0]](*[int(digit) for digit in chain.tag[1:] or "0"])

    return held["out"][None]


ORDER = ("A0", "A1", "B0:0.5", "Q", "B1", "C0:0.5", "B2", "G", "C1", "T1", "T0", "D0", "E0", "C2", "S0", "D1", "F0:0.5", "E1", "T2", "D2", "E20", "S1", "F1", "Z0:3", "E21", "S20", "S21", "E22", "F20", "S22", "Z1", "F21", "F22", "Z20", "Z21", "Z22:0.5")


def solution(mesh):
    in_specs = (
        P("leaf", None, None),
        P("shift", "leaf", None, None),
        P("shift", "leaf", None, None),
        P("leaf", None),
        P(),
        P("shift", None, "leaf", None, None),
        P("shift", None, "leaf", None, None),
        P("shift"),
    )
    out_specs = P("leaf", "shift", None)
    return jax.shard_map(body, mesh=mesh, in_specs=in_specs, out_specs=out_specs, check_vma=False)
```

```python
import functools

import jax
import jax.numpy as jnp
from jax import lax
from jax.experimental import pallas as pl
from jax.experimental.pallas import tpu as pltpu
from jax.sharding import PartitionSpec as P

WIDE = jnp.float32
NARROW = jnp.bfloat16
VMEM_LIMIT = 16 * 1024 * 1024
SHARES = (1, 1, 2)
GROUPS = ((0, 1), (2,))
PARTS = ((((0, 0, 1), (1, 0, 1)),), (((0, 0, 1), (1, 0, 1)),), (((0, 0, 2),), ((1, 0, 1),), ((1, 1, 1),)))
COST = 0.01
TILES = 4


def exchange(value, axis, bit):
    mask = 2**bit
    pairs = [(source, source ^ mask) for source in range(lax.axis_size(axis))]
    return lax.ppermute(value, axis, pairs)


def dot(left, right, left_dim=1, right_dim=0):
    return lax.dot_general(
        left, right, (((left_dim,), (right_dim,)), ((), ())), preferred_element_type=WIDE
    )


class Chain:
    def __init__(self):
        self.last = None
        self.tag = None
        self.cost = COST

    def __call__(self, kernel, outs, scalars, arrays, name, far=(), spaces=None, scratch=(), place=None):
        after = [] if self.last is None else [self.last]
        spaces = spaces or [pltpu.VMEM] * len(outs)
        taken = [] if place is None else [place]
        aliases = {len(after) + len(scalars) + len(arrays): 0} if taken else {}

        def run(*refs):
            kernel(*refs[len(after) :])

        results = pl.pallas_call(
            run,
            out_shape=[jax.ShapeDtypeStruct(shape, kind) for shape, kind in outs],
            in_specs=[pl.BlockSpec(memory_space=pl.ANY)] * len(after)
            + [pl.BlockSpec(memory_space=pltpu.SMEM)] * len(scalars)
            + [pl.BlockSpec(memory_space=pltpu.VMEM)] * len(arrays)
            + [pl.BlockSpec(memory_space=pltpu.HBM)] * len(taken)
            + [pl.BlockSpec(memory_space=pl.ANY)] * len(far),
            out_specs=[pl.BlockSpec(memory_space=space) for space in spaces],
            input_output_aliases=aliases,
            scratch_shapes=scratch,
            cost_estimate=pl.CostEstimate(
                flops=int(self.cost * 1.15e9), bytes_accessed=1, transcendentals=0
            ),
            compiler_params=pltpu.CompilerParams(vmem_limit_bytes=VMEM_LIMIT),
            name=self.tag + "_" + name,
        )(*after, *scalars, *arrays, *taken, *[pltpu.with_memory_space_constraint(a, pltpu.HBM) for a in far])
        self.last = results[-1]
        return results


def selector(rows, front):
    at = lax.broadcasted_iota(jnp.int32, (front, rows.shape[1]), 0)
    return (at == rows[...]).astype(WIDE).astype(NARROW)


def load_kernel(masks, width, rhs_in, inverse_in, coupling_in, rows_in, fronts_in, links_in, *refs):
    own, other, half, chosen, inverse, mixed, coupling, rhs, front, link, rows, sems = refs
    count = rhs.shape[1] // 2
    block = inverse.shape[0] // len(masks)
    core = lax.axis_index("leaf") & 1
    shift = lax.axis_index("shift")
    copies = []

    def load(source, target):
        copies.append(pltpu.make_async_copy(source, target, sems.at[len(copies)]))
        copies[-1].start()
        return copies[-1]

    def load_columns(start, size):
        return [
            load(
                rhs_in.at[:, pl.ds(pl.multiple_of(side * count + start, 128), size)],
                rhs.at[:, pl.ds(number * count + start, size)],
            )
            for number, side in enumerate((core, 1 - core))
        ]

    def load_blocks(source, target):
        return [
            load(
                source.at[pl.ds(pl.multiple_of((shift ^ mask) * block, block), block)],
                target.at[pl.ds(number * block, block)],
            )
            for number, mask in enumerate(masks)
        ]

    row_copy = load(rows_in, rows)
    first = load_columns(0, width)
    blocks = load_blocks(inverse_in, inverse)
    small = load_blocks(coupling_in, mixed)
    row_copy.wait()
    selected = selector(rows, own.shape[1])
    chosen[...] = selected

    for copy in first:
        copy.wait()
    both = jnp.concatenate([rhs[:, :width], rhs[:, count : count + width]], axis=1)
    parts = TILES
    for part in range(parts):
        for copy in blocks[part * len(blocks) // parts : (part + 1) * len(blocks) // parts]:
            copy.wait()
        if part == 0:
            later = [load(fronts_in.at[0], front), load(links_in.at[0], link), load(coupling_in, coupling)]
            if width < count:
                later += load_columns(width, count - width)
        tile = pl.ds(part * (inverse.shape[0] // parts), inverse.shape[0] // parts)
        half[tile, :] = dot(inverse[tile, :], both).astype(NARROW)
    for copy in small:
        copy.wait()
    boundary = dot(half[...], mixed[...], 0, 0).astype(NARROW)
    placed = dot(boundary, chosen[...], 1, 1).astype(NARROW)
    own[...] = placed[:width]
    other[...] = placed[width:]
    for copy in later:
        copy.wait()


def leaf_up_kernel(offset, width, inverse, rhs, mixed, chosen, *refs):
    if len(refs) > 3:
        fronts_in, links_in, own, other, half, fronts, links, sems = refs
        copies = [
            pltpu.make_async_copy(source.at[pl.ds(1, target.shape[0])], target, sems.at[number])
            for number, (source, target) in enumerate(((fronts_in, fronts), (links_in, links)))
        ]
    else:
        own, other, half = refs
        copies = []
    for copy in copies:
        copy.start()
    count = rhs.shape[1] // 2
    both = jnp.concatenate(
        [rhs[:, offset : offset + width], rhs[:, count + offset : count + offset + width]], axis=1
    )
    product = dot(inverse[...], both).astype(NARROW)
    half[...] = product
    boundary = dot(product, mixed[...], 0, 0).astype(NARROW)
    placed = dot(boundary, chosen[...], 1, 1).astype(NARROW)
    own[...] = placed[:width]
    other[...] = placed[width:]
    for copy in copies:
        copy.wait()


def gather(level, mine, received, alive):
    total = mine.astype(WIDE) + received.astype(WIDE)
    return (total * alive[level : level + 1, :]).astype(NARROW)


def front_up_kernel(at, alive, mine, received, front, link, carried, solved):
    rows = pl.ds(at, carried.shape[0])
    operand = gather(0, mine[rows], received[rows], alive)
    result = (dot(operand, front[...], 1, 1) * alive[0:1, :]).astype(NARROW)
    solved[...] = result
    carried[...] = dot(result, link[...]).astype(NARROW)


def product_kernel(alive, front, link, fronts, links, downs, ups):
    across = alive[...].T
    for level in range(links.shape[0]):
        coupling = links[level]
        masked = (coupling.astype(WIDE) * across[:, level + 1 : level + 2]).astype(NARROW)
        ups[level] = dot(fronts[level], masked, 0, 0).astype(NARROW)
        downs[level + 1] = dot(fronts[level], coupling).astype(NARROW)
    downs[0] = dot(front[...], link[...]).astype(NARROW)


def front_pass_kernel(level, alive, mine, received, ups, carried, operand):
    value = gather(level, mine[...], received[...], alive)
    operand[...] = value
    carried[...] = dot(value, ups[level - 1]).astype(NARROW)


def front_solve_kernel(level, alive, operand, fronts, solved):
    solved[...] = (dot(operand[...], fronts[level - 1], 1, 1) * alive[level : level + 1, :]).astype(NARROW)


def top_kernel(levels, alive, mine, received, fronts, downs, *refs):
    *solved, back = refs
    operand = gather(levels - 1, mine[...], received[...], alive)
    current = (dot(operand, fronts[levels - 2], 1, 1) * alive[levels - 1 : levels, :]).astype(NARROW)
    for level in range(levels - 2, -1, -1):
        correction = dot(current, downs[level], 1, 1)
        value = solved[level][...].astype(WIDE) - correction
        current = (value * alive[level : level + 1, :]).astype(NARROW)
    back[...] = current


def lift_kernel(inverse, coupling, scale, lift):
    lift[...] = (dot(inverse[...], coupling[...]) * scale[0:1, 0:1]).astype(NARROW)


def down(first, spans, scale, lift, picked, half, out):
    size = out.shape[0]
    rows = pl.ds(0 if first else half.shape[0] - size, size)
    halves = jnp.concatenate([half[rows, pl.ds(at, width)] for at, width in spans], axis=1)
    result = halves.astype(WIDE) * scale[0:1, 0:1] - dot(lift[rows, :], picked, 1, 1)
    out[...] = result.astype(out.dtype)


def down_first_kernel(spans, rows, scale, lift, chosen, half, *refs):
    *backs, out, picked = refs
    back = jnp.concatenate([ref[pl.ds(at, width)] for ref, (at, width) in zip(backs, rows)], axis=0)
    values = dot(back, chosen[...]).astype(NARROW)
    picked[...] = values
    down(True, spans, scale, lift, values, half, out)


def down_second_kernel(spans, scale, lift, half, picked, out):
    down(False, spans, scale, lift, picked[...], half, out)


def add_kernel(kept, came, sent, rest):
    total = kept[...] + came[...].astype(WIDE)
    rows = sent.shape[0]
    sent[...] = total[:rows].astype(NARROW)
    rest[...] = total[rows:]


def finish_kernel(spans, kept, came, *refs):
    out, token, total, sems = refs[-4:]
    count = out.shape[1] // 2
    core = lax.axis_index("leaf") & 1
    total[...] = kept[...] + came[...].astype(WIDE)
    token[...] = jnp.zeros_like(token)
    copies, at = [], 0
    for number, (side, start, width) in enumerate(spans):
        column = (core if side == 0 else 1 - core) * count + start
        target = out.at[:, pl.ds(pl.multiple_of(column, 128), width)]
        copies.append(pltpu.make_async_copy(total.at[:, pl.ds(at, width)], target, sems.at[number]))
        copies[-1].start()
        at += width
    for copy in copies:
        copy.wait()


def body(
    leaf_rhs,
    leaf_inverse,
    leaf_coupling,
    leaf_rows,
    front_sizes,
    front_inverse,
    front_coupling,
    shift_weight,
):
    levels = lax.axis_size("leaf").bit_length() - 1
    shifts = lax.axis_size("shift")
    steps = shifts.bit_length() - 1
    inverse_in, coupling_in, rhs_in = leaf_inverse[0, 0], leaf_coupling[0, 0], leaf_rhs[0]
    fronts_in, links_in = front_inverse[0, :, 0], front_coupling[0, :, 0]
    order, columns = rhs_in.shape
    front, boundary = fronts_in.shape[-1], coupling_in.shape[1]
    block = order // shifts
    unit = columns // (2 * sum(SHARES))
    widths = [share * unit for share in SHARES]
    offsets = [sum(widths[:n]) for n in range(len(widths))]
    def masks_of(step):
        if step == steps:
            return [0]
        stay = masks_of(step + 1)
        return [m | 1 << step for m in stay] + stay
    stay = masks_of(1)
    leave = [m | 1 for m in stay]

    chain = Chain()
    state = [dict() for _ in widths]
    final = [None for _ in widths]

    unknowns = jnp.arange(front, dtype=jnp.int32)[None, :]
    sizes = jnp.pad(front_sizes, (0, 8 - levels % 8))[:, None]
    held = {
        "alive": (unknowns < sizes).astype(WIDE),
        "scale": jnp.broadcast_to(shift_weight, (8, 128)).astype(WIDE),
    }

    unknowns = jnp.arange(front, dtype=jnp.int32)[None, :]
    sizes = jnp.pad(front_sizes, (0, 8 - levels % 8))[:, None]
    held = {
        "alive": (unknowns < sizes).astype(WIDE),
        "scale": jnp.broadcast_to(shift_weight, (8, 128)).astype(WIDE),
    }

    unknowns = jnp.arange(front, dtype=jnp.int32)[None, :]
    sizes = jnp.pad(front_sizes, (0, 8 - levels % 8))[:, None]
    held = {
        "alive": (unknowns < sizes).astype(WIDE),
        "scale": jnp.broadcast_to(shift_weight, (8, 128)).astype(WIDE),
    }

    def leaf(group):
        chunks = GROUPS[group]
        offset, width = offsets[chunks[0]], sum(widths[n] for n in chunks)
        outs = [((width, front), NARROW)] * 2 + [((order, 2 * width), NARROW)]
        if group == 0:
            shapes = [inverse_in.shape, coupling_in.shape, coupling_in.shape, rhs_in.shape, (front, front), (front, front)]
            names = ["chosen", "inverse", "mixed", "coupling", "rhs", "front", "link"]
            own, other, half, *loaded = chain(
                functools.partial(load_kernel, (*leave, *stay), width),
                [*outs, ((front, boundary), NARROW), *[(shape, NARROW) for shape in shapes]],
                [], [], "leaf_up",
                far=[rhs_in, inverse_in, coupling_in, leaf_rows, fronts_in, links_in],
                scratch=[
                    pltpu.VMEM(leaf_rows.shape, jnp.int32),
                    pltpu.SemaphoreType.DMA((10 + 2 * shifts,)),
                ],
            )
            held.update(zip(names, loaded))
        else:
            far = [fronts_in, links_in] if group == 1 else []
            outs += [((a.shape[0] - 1, front, front), NARROW) for a in far]
            own, other, half, *loaded = chain(
                functools.partial(leaf_up_kernel, offset, width), outs, [],
                [held[k] for k in ("inverse", "rhs", "mixed", "chosen")], "leaf_up",
                far=far, scratch=[pltpu.SemaphoreType.DMA((2,))] if far else [],
            )
            held.update(zip(("fronts", "links"), loaded))
        came = exchange(other, "leaf", 0)
        for n in chunks:
            at = offsets[n] - offset
            state[n].update(mine=own, came=came, half=half, solved=[], at=at, spans=(at, width + at))

    def up(n):
        width = widths[n]
        s = state[n]
        s["mine"], solved = chain(
            functools.partial(front_up_kernel, s["at"]), [((width, front), NARROW)] * 2, [],
            [held["alive"], s["mine"], s["came"], held["front"], held["link"]], "front_up",
        )
        s["solved"].append(solved)
        s["came"] = exchange(s["mine"], "leaf", 1)

    def products():
        held["downs"], held["ups"] = chain(
            product_kernel,
            [((levels - 1, front, front), NARROW), ((levels - 2, front, front), NARROW)],
            [], [held[k] for k in ("alive", "front", "link", "fronts", "links")], "products",
        )

    def middle(n):
        s = state[n]
        s["operands"] = []
        for level in range(1, levels - 1):
            s["mine"], operand = chain(
                functools.partial(front_pass_kernel, level), [((widths[n], front), NARROW)] * 2, [],
                [held["alive"], s["mine"], s["came"], held["ups"]], "front_pass",
            )
            s["operands"].append(operand)
            s["came"] = exchange(s["mine"], "leaf", level + 1)

    def solve(n):
        s = state[n]
        for level in range(1, levels - 1):
            s["solved"] += chain(
                functools.partial(front_solve_kernel, level), [((widths[n], front), NARROW)], [],
                [held["alive"], s["operands"][level - 1], held["fronts"]], "front_solve",
            )

    def top(n):
        s = state[n]
        (s["back"],) = chain(
            functools.partial(top_kernel, levels), [((widths[n], front), NARROW)], [],
            [held["alive"], s["mine"], s["came"], held["fronts"], held["downs"], *s["solved"]], "top",
        )
        s["back_came"] = exchange(s["back"], "leaf", 0)

    def lift():
        (held["lift"],) = chain(
            lift_kernel, [((order, boundary), NARROW)], [],
            [held["inverse"], held["coupling"], held["scale"]], "lift",
        )

    def pieces(n, part=0):
        spans = [(side, start * unit, width * unit) for side, start, width in PARTS[n][part]]
        return spans, sum(width for _, _, width in spans)

    def first(n, part=0):
        s = state[n]
        spans, width = pieces(n, part)
        inside = tuple((s["spans"][side] + start, size) for side, start, size in spans)
        sent, s["picked", part] = chain(
            functools.partial(down_first_kernel, inside, tuple(span[1:] for span in spans)),
            [((len(leave) * block, width), NARROW), ((width, boundary), NARROW)],
            [],
            [held["scale"], held["lift"], held["chosen"], s["half"], *[s["back_came" if side else "back"] for side, _, _ in spans]],
            "down_first",
        )
        s["sum_came", part] = exchange(sent, "shift", 0)

    def second(n, part=0):
        s = state[n]
        spans, width = pieces(n, part)
        inside = tuple((s["spans"][side] + start, size) for side, start, size in spans)
        (s["kept", part],) = chain(
            functools.partial(down_second_kernel, inside),
            [((len(stay) * block, width), WIDE)],
            [],
            [held["scale"], held["lift"], s["half"], s["picked", part]],
            "down_second",
        )

    def add(n, part=0):
        s = state[n]
        _, width = pieces(n, part)
        for step in range(1, steps):
            rows = block * (shifts >> step + 1)
            sent, s["kept", part] = chain(
                add_kernel, [((rows, width), NARROW), ((rows, width), WIDE)], [],
                [s["kept", part], s["sum_came", part]], "add",
            )
            s["sum_came", part] = exchange(sent, "shift", step)

    def last(n, part=0):
        s = state[n]
        spans, width = pieces(n, part)
        targets = tuple((side, offsets[n] + start, size) for side, start, size in spans)
        held["out"], _ = chain(
            functools.partial(finish_kernel, targets), [((block, columns), WIDE), ((8, 128), WIDE)], [],
            [s["kept", part], s["sum_came", part]], "finish", place=held.get("out"),
            spaces=[pltpu.HBM, pltpu.VMEM],
            scratch=[pltpu.VMEM((block, width), WIDE), pltpu.SemaphoreType.DMA((len(spans),))],
        )

    run = {
        "A": leaf,
        "B": up,
        "C": middle,
        "T": solve,
        "Q": lambda n: products(),
        "D": top,
        "G": lambda n: lift(),
        "E": first,
        "S": second,
        "F": add,
        "Z": last,
    }
    for step in ORDER:
        chain.tag, _, cost = step.partition(":")
        chain.cost = float(cost or COST)
        run[step[0]](*[int(digit) for digit in chain.tag[1:] or "0"])

    return held["out"][None]


ORDER = ("A0", "A1", "B0:0.5", "Q", "B1", "C0:0.5", "B2", "G", "C1", "T1", "T0", "D0", "E0", "C2", "S0", "D1", "F0:0.5", "E1", "T2", "D2", "E20", "S1", "F1", "Z0:3", "E21", "S20", "S21", "E22", "F20", "S22", "Z1", "F21", "F22", "Z20", "Z21", "Z22:0.5")


def solution(mesh):
    in_specs = (
        P("leaf", None, None),
        P("shift", "leaf", None, None),
        P("shift", "leaf", None, None),
        P("leaf", None),
        P(),
        P("shift", None, "leaf", None, None),
        P("shift", None, "leaf", None, None),
        P("shift"),
    )
    out_specs = P("leaf", "shift", None)
    return jax.shard_map(body, mesh=mesh, in_specs=in_specs, out_specs=out_specs, check_vma=False)
```

```python
import functools

import jax
import jax.numpy as jnp
from jax import lax
from jax.experimental import pallas as pl
from jax.experimental.pallas import tpu as pltpu
from jax.sharding import PartitionSpec as P

WIDE = jnp.float32
NARROW = jnp.bfloat16
VMEM_LIMIT = 16 * 1024 * 1024
SHARES = (1, 1, 2)
GROUPS = ((0, 1), (2,))
PARTS = ((((0, 0, 1), (1, 0, 1)),), (((0, 0, 1), (1, 0, 1)),), (((0, 0, 2),), ((1, 0, 1),), ((1, 1, 1),)))
COST = 0.01
TILES = 4


def exchange(value, axis, bit):
    mask = 2**bit
    pairs = [(source, source ^ mask) for source in range(lax.axis_size(axis))]
    return lax.ppermute(value, axis, pairs)


def dot(left, right, left_dim=1, right_dim=0):
    return lax.dot_general(
        left, right, (((left_dim,), (right_dim,)), ((), ())), preferred_element_type=WIDE
    )


class Chain:
    def __init__(self):
        self.last = None
        self.tag = None
        self.cost = COST

    def __call__(self, kernel, outs, scalars, arrays, name, far=(), spaces=None, scratch=(), place=None):
        after = [] if self.last is None else [self.last]
        spaces = spaces or [pltpu.VMEM] * len(outs)
        taken = [] if place is None else [place]
        aliases = {len(after) + len(scalars) + len(arrays): 0} if taken else {}

        def run(*refs):
            kernel(*refs[len(after) :])

        results = pl.pallas_call(
            run,
            out_shape=[jax.ShapeDtypeStruct(shape, kind) for shape, kind in outs],
            in_specs=[pl.BlockSpec(memory_space=pl.ANY)] * len(after)
            + [pl.BlockSpec(memory_space=pltpu.SMEM)] * len(scalars)
            + [pl.BlockSpec(memory_space=pltpu.VMEM)] * len(arrays)
            + [pl.BlockSpec(memory_space=pltpu.HBM)] * len(taken)
            + [pl.BlockSpec(memory_space=pl.ANY)] * len(far),
            out_specs=[pl.BlockSpec(memory_space=space) for space in spaces],
            input_output_aliases=aliases,
            scratch_shapes=scratch,
            cost_estimate=pl.CostEstimate(
                flops=int(self.cost * 1.15e9), bytes_accessed=1, transcendentals=0
            ),
            compiler_params=pltpu.CompilerParams(vmem_limit_bytes=VMEM_LIMIT),
            name=self.tag + "_" + name,
        )(*after, *scalars, *arrays, *taken, *[pltpu.with_memory_space_constraint(a, pltpu.HBM) for a in far])
        self.last = results[-1]
        return results


def selector(rows, front):
    at = lax.broadcasted_iota(jnp.int32, (front, rows.shape[1]), 0)
    return (at == rows[...]).astype(WIDE).astype(NARROW)


def load_kernel(masks, width, rhs_in, inverse_in, coupling_in, rows_in, fronts_in, links_in, *refs):
    own, other, half, chosen, inverse, mixed, coupling, rhs, front, link, rows, sems = refs
    count = rhs.shape[1] // 2
    block = inverse.shape[0] // len(masks)
    core = lax.axis_index("leaf") & 1
    shift = lax.axis_index("shift")
    copies = []

    def load(source, target):
        copies.append(pltpu.make_async_copy(source, target, sems.at[len(copies)]))
        copies[-1].start()
        return copies[-1]

    def load_columns(start, size):
        return [
            load(
                rhs_in.at[:, pl.ds(pl.multiple_of(side * count + start, 128), size)],
                rhs.at[:, pl.ds(number * count + start, size)],
            )
            for number, side in enumerate((core, 1 - core))
        ]

    def load_blocks(source, target):
        return [
            load(
                source.at[pl.ds(pl.multiple_of((shift ^ mask) * block, block), block)],
                target.at[pl.ds(number * block, block)],
            )
            for number, mask in enumerate(masks)
        ]

    first = load_columns(0, width)
    blocks = load_blocks(inverse_in, inverse)
    small = [load(rows_in, rows)]
    small += load_blocks(coupling_in, mixed)

    for copy in first:
        copy.wait()
    both = jnp.concatenate([rhs[:, :width], rhs[:, count : count + width]], axis=1)
    parts = TILES
    for part in range(parts):
        for copy in blocks[part * len(blocks) // parts : (part + 1) * len(blocks) // parts]:
            copy.wait()
        if part == 0:
            later = [load(fronts_in.at[0], front), load(links_in.at[0], link), load(coupling_in, coupling)]
            if width < count:
                later += load_columns(width, count - width)
        tile = pl.ds(part * (inverse.shape[0] // parts), inverse.shape[0] // parts)
        half[tile, :] = dot(inverse[tile, :], both).astype(NARROW)
    for copy in small:
        copy.wait()
    selected = selector(rows, own.shape[1])
    chosen[...] = selected
    boundary = dot(half[...], mixed[...], 0, 0).astype(NARROW)
    placed = dot(boundary, selected, 1, 1).astype(NARROW)
    own[...] = placed[:width]
    other[...] = placed[width:]
    for copy in later:
        copy.wait()


def leaf_up_kernel(offset, width, inverse, rhs, mixed, chosen, *refs):
    if len(refs) > 3:
        fronts_in, links_in, own, other, half, fronts, links, sems = refs
        copies = [
            pltpu.make_async_copy(source.at[pl.ds(1, target.shape[0])], target, sems.at[number])
            for number, (source, target) in enumerate(((fronts_in, fronts), (links_in, links)))
        ]
    else:
        own, other, half = refs
        copies = []
    for copy in copies:
        copy.start()
    count = rhs.shape[1] // 2
    both = jnp.concatenate(
        [rhs[:, offset : offset + width], rhs[:, count + offset : count + offset + width]], axis=1
    )
    product = dot(inverse[...], both).astype(NARROW)
    half[...] = product
    boundary = dot(product, mixed[...], 0, 0).astype(NARROW)
    placed = dot(boundary, chosen[...], 1, 1).astype(NARROW)
    own[...] = placed[:width]
    other[...] = placed[width:]
    for copy in copies:
        copy.wait()


def gather(level, mine, received, alive):
    total = mine.astype(WIDE) + received.astype(WIDE)
    return (total * alive[level : level + 1, :]).astype(NARROW)


def front_up_kernel(at, alive, mine, received, front, link, carried, solved):
    rows = pl.ds(at, carried.shape[0])
    operand = gather(0, mine[rows], received[rows], alive)
    result = (dot(operand, front[...], 1, 1) * alive[0:1, :]).astype(NARROW)
    solved[...] = result
    carried[...] = dot(result, link[...]).astype(NARROW)


def product_kernel(alive, front, link, fronts, links, downs, ups):
    across = alive[...].T
    for level in range(links.shape[0]):
        coupling = links[level]
        masked = (coupling.astype(WIDE) * across[:, level + 1 : level + 2]).astype(NARROW)
        ups[level] = dot(fronts[level], masked, 0, 0).astype(NARROW)
        downs[level + 1] = dot(fronts[level], coupling).astype(NARROW)
    downs[0] = dot(front[...], link[...]).astype(NARROW)


def front_pass_kernel(level, alive, mine, received, ups, carried, operand):
    value = gather(level, mine[...], received[...], alive)
    operand[...] = value
    carried[...] = dot(value, ups[level - 1]).astype(NARROW)


def front_solve_kernel(level, alive, operand, fronts, solved):
    solved[...] = (dot(operand[...], fronts[level - 1], 1, 1) * alive[level : level + 1, :]).astype(NARROW)


def top_kernel(levels, alive, mine, received, fronts, downs, *refs):
    *solved, back = refs
    operand = gather(levels - 1, mine[...], received[...], alive)
    current = (dot(operand, fronts[levels - 2], 1, 1) * alive[levels - 1 : levels, :]).astype(NARROW)
    for level in range(levels - 2, -1, -1):
        correction = dot(current, downs[level], 1, 1)
        value = solved[level][...].astype(WIDE) - correction
        current = (value * alive[level : level + 1, :]).astype(NARROW)
    back[...] = current


def lift_kernel(inverse, coupling, scale, lift):
    lift[...] = (dot(inverse[...], coupling[...]) * scale[0:1, 0:1]).astype(NARROW)


def down(first, spans, scale, lift, picked, half, out):
    size = out.shape[0]
    rows = pl.ds(0 if first else half.shape[0] - size, size)
    halves = jnp.concatenate([half[rows, pl.ds(at, width)] for at, width in spans], axis=1)
    result = halves.astype(WIDE) * scale[0:1, 0:1] - dot(lift[rows, :], picked, 1, 1)
    out[...] = result.astype(out.dtype)


def down_first_kernel(spans, rows, scale, lift, chosen, half, *refs):
    *backs, out, picked = refs
    back = jnp.concatenate([ref[pl.ds(at, width)] for ref, (at, width) in zip(backs, rows)], axis=0)
    values = dot(back, chosen[...]).astype(NARROW)
    picked[...] = values
    down(True, spans, scale, lift, values, half, out)


def down_second_kernel(spans, scale, lift, half, picked, out):
    down(False, spans, scale, lift, picked[...], half, out)


def add_kernel(kept, came, sent, rest):
    total = kept[...] + came[...].astype(WIDE)
    rows = sent.shape[0]
    sent[...] = total[:rows].astype(NARROW)
    rest[...] = total[rows:]


def finish_kernel(spans, kept, came, *refs):
    out, token, total, sems = refs[-4:]
    count = out.shape[1] // 2
    core = lax.axis_index("leaf") & 1
    total[...] = kept[...] + came[...].astype(WIDE)
    token[...] = jnp.zeros_like(token)
    copies, at = [], 0
    for number, (side, start, width) in enumerate(spans):
        column = (core if side == 0 else 1 - core) * count + start
        target = out.at[:, pl.ds(pl.multiple_of(column, 128), width)]
        copies.append(pltpu.make_async_copy(total.at[:, pl.ds(at, width)], target, sems.at[number]))
        copies[-1].start()
        at += width
    for copy in copies:
        copy.wait()


def body(
    leaf_rhs,
    leaf_inverse,
    leaf_coupling,
    leaf_rows,
    front_sizes,
    front_inverse,
    front_coupling,
    shift_weight,
):
    levels = lax.axis_size("leaf").bit_length() - 1
    shifts = lax.axis_size("shift")
    steps = shifts.bit_length() - 1
    inverse_in, coupling_in, rhs_in = leaf_inverse[0, 0], leaf_coupling[0, 0], leaf_rhs[0]
    fronts_in, links_in = front_inverse[0, :, 0], front_coupling[0, :, 0]
    order, columns = rhs_in.shape
    front, boundary = fronts_in.shape[-1], coupling_in.shape[1]
    block = order // shifts
    unit = columns // (2 * sum(SHARES))
    widths = [share * unit for share in SHARES]
    offsets = [sum(widths[:n]) for n in range(len(widths))]
    def masks_of(step):
        if step == steps:
            return [0]
        stay = masks_of(step + 1)
        return [m | 1 << step for m in stay] + stay
    stay = masks_of(1)
    leave = [m | 1 for m in stay]

    chain = Chain()
    state = [dict() for _ in widths]
    final = [None for _ in widths]

    unknowns = jnp.arange(front, dtype=jnp.int32)[None, :]
    sizes = jnp.pad(front_sizes, (0, 8 - levels % 8))[:, None]
    held = {
        "alive": (unknowns < sizes).astype(WIDE),
        "scale": jnp.broadcast_to(shift_weight, (8, 128)).astype(WIDE),
    }

    unknowns = jnp.arange(front, dtype=jnp.int32)[None, :]
    sizes = jnp.pad(front_sizes, (0, 8 - levels % 8))[:, None]
    held = {
        "alive": (unknowns < sizes).astype(WIDE),
        "scale": jnp.broadcast_to(shift_weight, (8, 128)).astype(WIDE),
    }

    unknowns = jnp.arange(front, dtype=jnp.int32)[None, :]
    sizes = jnp.pad(front_sizes, (0, 8 - levels % 8))[:, None]
    held = {
        "alive": (unknowns < sizes).astype(WIDE),
        "scale": jnp.broadcast_to(shift_weight, (8, 128)).astype(WIDE),
    }

    def leaf(group):
        chunks = GROUPS[group]
        offset, width = offsets[chunks[0]], sum(widths[n] for n in chunks)
        outs = [((width, front), NARROW)] * 2 + [((order, 2 * width), NARROW)]
        if group == 0:
            shapes = [inverse_in.shape, coupling_in.shape, coupling_in.shape, rhs_in.shape, (front, front), (front, front)]
            names = ["chosen", "inverse", "mixed", "coupling", "rhs", "front", "link"]
            own, other, half, *loaded = chain(
                functools.partial(load_kernel, (*leave, *stay), width),
                [*outs, ((front, boundary), NARROW), *[(shape, NARROW) for shape in shapes]],
                [], [], "leaf_up",
                far=[rhs_in, inverse_in, coupling_in, leaf_rows, fronts_in, links_in],
                scratch=[
                    pltpu.VMEM(leaf_rows.shape, jnp.int32),
                    pltpu.SemaphoreType.DMA((10 + 2 * shifts,)),
                ],
            )
            held.update(zip(names, loaded))
        else:
            far = [fronts_in, links_in] if group == 1 else []
            outs += [((a.shape[0] - 1, front, front), NARROW) for a in far]
            own, other, half, *loaded = chain(
                functools.partial(leaf_up_kernel, offset, width), outs, [],
                [held[k] for k in ("inverse", "rhs", "mixed", "chosen")], "leaf_up",
                far=far, scratch=[pltpu.SemaphoreType.DMA((2,))] if far else [],
            )
            held.update(zip(("fronts", "links"), loaded))
        came = exchange(other, "leaf", 0)
        for n in chunks:
            at = offsets[n] - offset
            state[n].update(mine=own, came=came, half=half, solved=[], at=at, spans=(at, width + at))

    def up(n):
        width = widths[n]
        s = state[n]
        s["mine"], solved = chain(
            functools.partial(front_up_kernel, s["at"]), [((width, front), NARROW)] * 2, [],
            [held["alive"], s["mine"], s["came"], held["front"], held["link"]], "front_up",
        )
        s["solved"].append(solved)
        s["came"] = exchange(s["mine"], "leaf", 1)

    def products():
        held["downs"], held["ups"] = chain(
            product_kernel,
            [((levels - 1, front, front), NARROW), ((levels - 2, front, front), NARROW)],
            [], [held[k] for k in ("alive", "front", "link", "fronts", "links")], "products",
        )

    def middle(n):
        s = state[n]
        s["operands"] = []
        for level in range(1, levels - 1):
            s["mine"], operand = chain(
                functools.partial(front_pass_kernel, level), [((widths[n], front), NARROW)] * 2, [],
                [held["alive"], s["mine"], s["came"], held["ups"]], "front_pass",
            )
            s["operands"].append(operand)
            s["came"] = exchange(s["mine"], "leaf", level + 1)

    def solve(n):
        s = state[n]
        for level in range(1, levels - 1):
            s["solved"] += chain(
                functools.partial(front_solve_kernel, level), [((widths[n], front), NARROW)], [],
                [held["alive"], s["operands"][level - 1], held["fronts"]], "front_solve",
            )

    def top(n):
        s = state[n]
        (s["back"],) = chain(
            functools.partial(top_kernel, levels), [((widths[n], front), NARROW)], [],
            [held["alive"], s["mine"], s["came"], held["fronts"], held["downs"], *s["solved"]], "top",
        )
        s["back_came"] = exchange(s["back"], "leaf", 0)

    def lift():
        (held["lift"],) = chain(
            lift_kernel, [((order, boundary), NARROW)], [],
            [held["inverse"], held["coupling"], held["scale"]], "lift",
        )

    def pieces(n, part=0):
        spans = [(side, start * unit, width * unit) for side, start, width in PARTS[n][part]]
        return spans, sum(width for _, _, width in spans)

    def first(n, part=0):
        s = state[n]
        spans, width = pieces(n, part)
        inside = tuple((s["spans"][side] + start, size) for side, start, size in spans)
        sent, s["picked", part] = chain(
            functools.partial(down_first_kernel, inside, tuple(span[1:] for span in spans)),
            [((len(leave) * block, width), NARROW), ((width, boundary), NARROW)],
            [],
            [held["scale"], held["lift"], held["chosen"], s["half"], *[s["back_came" if side else "back"] for side, _, _ in spans]],
            "down_first",
        )
        s["sum_came", part] = exchange(sent, "shift", 0)

    def second(n, part=0):
        s = state[n]
        spans, width = pieces(n, part)
        inside = tuple((s["spans"][side] + start, size) for side, start, size in spans)
        (s["kept", part],) = chain(
            functools.partial(down_second_kernel, inside),
            [((len(stay) * block, width), WIDE)],
            [],
            [held["scale"], held["lift"], s["half"], s["picked", part]],
            "down_second",
        )

    def add(n, part=0):
        s = state[n]
        _, width = pieces(n, part)
        for step in range(1, steps):
            rows = block * (shifts >> step + 1)
            sent, s["kept", part] = chain(
                add_kernel, [((rows, width), NARROW), ((rows, width), WIDE)], [],
                [s["kept", part], s["sum_came", part]], "add",
            )
            s["sum_came", part] = exchange(sent, "shift", step)

    def last(n, part=0):
        s = state[n]
        spans, width = pieces(n, part)
        targets = tuple((side, offsets[n] + start, size) for side, start, size in spans)
        held["out"], _ = chain(
            functools.partial(finish_kernel, targets), [((block, columns), WIDE), ((8, 128), WIDE)], [],
            [s["kept", part], s["sum_came", part]], "finish", place=held.get("out"),
            spaces=[pltpu.HBM, pltpu.VMEM],
            scratch=[pltpu.VMEM((block, width), WIDE), pltpu.SemaphoreType.DMA((len(spans),))],
        )

    run = {
        "A": leaf,
        "B": up,
        "C": middle,
        "T": solve,
        "Q": lambda n: products(),
        "D": top,
        "G": lambda n: lift(),
        "E": first,
        "S": second,
        "F": add,
        "Z": last,
    }
    for step in ORDER:
        chain.tag, _, cost = step.partition(":")
        chain.cost = float(cost or COST)
        run[step[0]](*[int(digit) for digit in chain.tag[1:] or "0"])

    return held["out"][None]


ORDER = ("A0", "A1", "B0:0.5", "Q", "B1", "C0:0.5", "B2", "G", "C1", "T1", "T0", "D0", "E0", "C2", "S0", "D1", "F0:0.5", "E1", "T2", "D2", "E20", "S1", "F1", "E21", "Z0:3", "S20", "S21", "E22", "F20", "S22", "Z1", "F21", "F22", "Z20", "Z21", "Z22:0.5")


def solution(mesh):
    in_specs = (
        P("leaf", None, None),
        P("shift", "leaf", None, None),
        P("shift", "leaf", None, None),
        P("leaf", None),
        P(),
        P("shift", None, "leaf", None, None),
        P("shift", None, "leaf", None, None),
        P("shift"),
    )
    out_specs = P("leaf", "shift", None)
    return jax.shard_map(body, mesh=mesh, in_specs=in_specs, out_specs=out_specs, check_vma=False)
```
